256 devices in a mesh: left: 8 (over x, z_hi), right: 32 (over y, z_lo, core).
Axes of the slice: x: 4, y: 4, z: 8 (z_hi: 2, z_lo: 4; z = z_hi * 4 + z_lo), core: 2. Of those that a mesh axis runs over, the one named last changes fastest.
Arguments:
- src_embed: float32 [98304, 400], P(('left', 'right')), may hold values from -1.5 to 1.5
- src_state: float32 [98304], P(('left', 'right')), may hold values from 0.002 to 0.05
- dst_embed: float32 [98304, 400], P(('left', 'right')), may hold values from -1.5 to 1.5
- dst_state: float32 [98304], P(('left', 'right')), may hold values from 0.002 to 0.05
- relation: float32 [256, 400], replicated, may hold values from -4 to 4
- rel_state: float32 [256, 400], replicated, may hold values from 5 to 50
- edge_src: int32 [256, 1000], P(('left', 'right')), may hold values from 0 to 383
- edge_dst: int32 [256, 1000], P(('left', 'right')), may hold values from 0 to 383
- edge_rel: int32 [256, 1000], P(('left', 'right')), may hold values from 0 to 255
- neg_rows: int32 [256, 2, 1000], P(('left', 'right')), may hold values from 0 to 383
- edge_count: int32 [256], P(('left', 'right')), may hold values from 250 to 1000, as said below
Outputs:
- src_out: float32 [98304, 400], P(('left', 'right'))
- dst_out: float32 [98304, 400], P(('left', 'right'))
- dst_state_out: float32 [98304], P(('left', 'right'))
- relation_out: float32 [256, 400], replicated
The draws below stay inside these ranges and needn't reach their ends.
Inputs may be any that keep to these rules, and one draw needn't show every extreme that they name: `edge_count`: each bucket's edge slots are live from the first one up to its count, the rest are padding; some bucket has all 1000 slots live.
All inputs are finite; a program needn't handle non-finite values.
Results may differ from the reference program's by a relative error of at most 0.0003.
Values sent between devices are 32-bit elements; how exact they have to be, the bound alone decides.
No kernel may reach another device: no remote copies, remote signals or barrier semaphores. Data moves between devices by JAX's collectives and lax.ppermute only.
A program may use at most 64 MiB of HBM per device.

```python
import math
import jax
import jax.numpy as jnp
import numpy as np
from jax import lax

W = 400
SLAB = 384
BATCH = 500
NEG = 1000
BATCHES = 2
REL = 256
SHIFT = 5
BLOCKS = 256
EDGES = 1000
N_LEFT = 8
N_RIGHT = 32


def draw_edge_count(key, part):
    key = jax.random.fold_in(key, 11)
    first_key, second_key = jax.random.split(key)
    counts = jax.random.randint(first_key, (BLOCKS,), EDGES // 4, EDGES + 1)
    chosen = jax.random.randint(second_key, (), 0, BLOCKS)
    filled = jnp.where(jnp.arange(BLOCKS) == chosen, EDGES, counts)
    return filled.astype(jnp.int32)


def place_ends(result, own_key, least, largest):
    place = [jax.random.randint(jax.random.fold_in(own_key, axis), (), 0, length) for axis, length in enumerate(result.shape)]
    widest = result.shape.index(max(result.shape))
    beside = place[:widest] + [(place[widest] + 1) % result.shape[widest]] + place[widest + 1:]
    return result.at[tuple(place)].set(least).at[tuple(beside)].set(largest)


def steps_of(rng, shape, shards, least, high):
    def one(axis_at, blocks):
        heights = jax.random.uniform(jax.random.fold_in(jax.random.fold_in(rng, 6), axis_at), (blocks,), jnp.float32, least / len(shards), high / len(shards))
        return jnp.repeat(jnp.exp(heights), shape[axis_at] // blocks).reshape((-1,) + (1,) * (len(shape) - axis_at - 1))

    level = one(*shards[0])
    for cut in shards[1:]:
        level = level * one(*cut)
    return level


def rank_table(count, skew):
    weights = [(1 << 20) // math.isqrt(rank ** skew) + 1 for rank in range(1, count + 1)]
    scale = 1 + sum(weights) // (1 << 30)
    return np.cumsum(np.array([max(1, weight // scale) for weight in weights]))


def ranked_ids(rng, extent, amount, skew):
    table = rank_table(amount, skew)
    pick = jax.random.randint(jax.random.fold_in(rng, 1), extent, 0, int(table[amount - 1]))
    rank = jnp.searchsorted(jnp.asarray(table, jnp.int32), pick, side="right")
    return jax.random.permutation(jax.random.fold_in(rng, 2), amount)[rank].astype(jnp.int32)


def scatter_about(own_key, shape, width, bound, shards=(), kind=jnp.bfloat16):
    level = steps_of(own_key, shape, shards, -0.22, 0.18) if shards else 1.0
    entries = jax.random.normal(own_key, shape, jnp.float32) * width * level
    return jnp.minimum(jnp.maximum(entries, -bound), bound).astype(kind)


def setup_inputs(seed: int = 0) -> dict:
    arg_keys = jax.random.split(jax.random.key(seed), 12)
    src_embed = scatter_about(arg_keys[0], (SLAB * BLOCKS, W), 0.25, 1.5, ((0, 256),), jnp.float32)
    src_state = jnp.clip(jnp.exp(math.log(0.05) - 3.218876 * jax.random.uniform(arg_keys[1], (SLAB * BLOCKS,), jnp.float32) ** steps_of(arg_keys[1], (SLAB * BLOCKS,), ((0, 256),), -0.2, 0.2)), 0.002, 0.05)
    dst_embed = scatter_about(arg_keys[2], (SLAB * BLOCKS, W), 0.25, 1.5, ((0, 256),), jnp.float32)
    dst_state = jnp.clip(jnp.exp(math.log(0.05) - 3.218876 * jax.random.uniform(arg_keys[3], (SLAB * BLOCKS,), jnp.float32) ** steps_of(arg_keys[3], (SLAB * BLOCKS,), ((0, 256),), -0.2, 0.2)), 0.002, 0.05)
    relation = scatter_about(arg_keys[4], (REL, W), 0.7, 4.0, (), jnp.float32)
    rel_state = jnp.clip(jnp.exp(jax.random.uniform(arg_keys[5], (REL, W), jnp.float32, math.log(5.0), math.log(50.0))), 5.0, 50.0)
    edge_src = place_ends(jax.random.randint(arg_keys[6], (BLOCKS, EDGES), 0, SLAB), jax.random.fold_in(arg_keys[6], 1), 0, SLAB - 1).astype(jnp.int32)
    edge_dst = place_ends(jax.random.randint(arg_keys[7], (BLOCKS, EDGES), 0, SLAB), jax.random.fold_in(arg_keys[7], 1), 0, SLAB - 1).astype(jnp.int32)
    edge_rel = place_ends(ranked_ids(arg_keys[8], (BLOCKS, EDGES), REL, 2), jax.random.fold_in(arg_keys[8], 3), 0, REL - 1).astype(jnp.int32)
    neg_rows = place_ends(jax.random.randint(arg_keys[9], (BLOCKS, BATCHES, NEG), 0, SLAB), jax.random.fold_in(arg_keys[9], 1), 0, SLAB - 1).astype(jnp.int32)
    edge_count = draw_edge_count(jax.random.fold_in(arg_keys[11], 71), 0)
    return dict(src_embed=src_embed, src_state=src_state, dst_embed=dst_embed, dst_state=dst_state, relation=relation, rel_state=rel_state, edge_src=edge_src, edge_dst=edge_dst, edge_rel=edge_rel, neg_rows=neg_rows, edge_count=edge_count)


ROW_RATE = 0.2
REL_RATE = 1.0

def complex_product(first, second):
    middle = first.shape[-1] // 2
    first_re, first_im = (first[:, :middle], first[:, middle:])
    second_re, second_im = (second[:, :middle], second[:, middle:])
    real_part = first_re * second_re - first_im * second_im
    imag_part = first_re * second_im + first_im * second_re
    return jnp.concatenate([real_part, imag_part], axis=-1)

def split_grads(query_grad, sources, relations):
    middle = sources.shape[-1] // 2
    grad_re, grad_im = (query_grad[:, :middle], query_grad[:, middle:])
    source_re, source_im = (sources[:, :middle], sources[:, middle:])
    rel_re, rel_im = (relations[:, :middle], relations[:, middle:])
    source_grad = jnp.concatenate([grad_re * rel_re + grad_im * rel_im, grad_im * rel_re - grad_re * rel_im], axis=-1)
    rho_grad = jnp.concatenate([grad_re * source_re + grad_im * source_im, grad_im * source_re - grad_re * source_im], axis=-1)
    return (source_grad, rho_grad)

def partner_side(queries, dst_rows, sample_rows, valid, table):
    targets = jnp.take(table, dst_rows, axis=0)
    samples = jnp.take(table, sample_rows, axis=0)
    positive = lax.optimization_barrier(jnp.sum(queries * targets, axis=-1))
    negative = jnp.dot(queries, samples.T, precision=lax.Precision.HIGHEST)
    pos_weight = -valid * jax.nn.sigmoid(-positive)
    neg_weight = valid[:, None] * jax.nn.sigmoid(negative) / samples.shape[0]
    query_grad = pos_weight[:, None] * targets + jnp.dot(neg_weight, samples, precision=lax.Precision.HIGHEST)
    sample_grad = jnp.dot(neg_weight.T, queries, precision=lax.Precision.HIGHEST)
    table_grad = jax.ops.segment_sum(pos_weight[:, None] * queries, dst_rows, num_segments=table.shape[0])
    table_grad = table_grad + jax.ops.segment_sum(sample_grad, sample_rows, num_segments=table.shape[0])
    return (query_grad, table_grad)

def entity_update(table, state, grad):
    new_state = state + lax.optimization_barrier(jnp.mean(grad * grad, axis=-1))
    return (table - ROW_RATE * grad / jnp.sqrt(new_state)[..., None], new_state)

def reference(src_embed, src_state, dst_embed, dst_state, relation, rel_state, edge_src, edge_dst, edge_rel, neg_rows, edge_count):
    blocks = N_LEFT * N_RIGHT
    numbers = jnp.arange(blocks, dtype=jnp.int32)
    partner = numbers // N_RIGHT * N_RIGHT + (numbers % N_RIGHT - SHIFT) % N_RIGHT
    inverse = numbers // N_RIGHT * N_RIGHT + (numbers % N_RIGHT + SHIFT) % N_RIGHT
    sources = src_embed.reshape(blocks, SLAB, W)
    source_state = src_state.reshape(blocks, SLAB)
    targets = dst_embed.reshape(blocks, SLAB, W)[partner]
    target_state = dst_state.reshape(blocks, SLAB)[partner]
    positions = jnp.arange(BATCH, dtype=jnp.int32)
    for batch_index in range(BATCHES):
        low = batch_index * BATCH

        def per_bucket(carry, items):
            src_table, dst_table, src_ids, dst_ids, rel_ids, sample_ids, live = items
            valid = (positions + low < live).astype(jnp.float32)
            source_rows = jnp.take(src_table, src_ids, axis=0)
            rel_rows = jnp.take(relation, rel_ids, axis=0)
            queries = complex_product(source_rows, rel_rows)
            query_grad, dst_grad = partner_side(queries, dst_ids, sample_ids, valid, dst_table)
            source_grad, rho_grad = split_grads(query_grad, source_rows, rel_rows)
            src_grad = jax.ops.segment_sum(source_grad, src_ids, num_segments=SLAB)
            carry = carry + jax.ops.segment_sum(rho_grad, rel_ids, num_segments=REL)
            return (carry, (src_grad, dst_grad))
        items = (sources, targets, edge_src[:, low:low + BATCH], edge_dst[:, low:low + BATCH], edge_rel[:, low:low + BATCH], neg_rows[:, batch_index], edge_count)
        rel_grad, grads = lax.scan(per_bucket, jnp.zeros((REL, W), jnp.float32), items)
        sources, source_state = entity_update(sources, source_state, grads[0])
        targets, target_state = entity_update(targets, target_state, grads[1])
        rel_state = rel_state + rel_grad * rel_grad
        relation = relation - REL_RATE * rel_grad / jnp.sqrt(rel_state)
    dst_out = targets[inverse].reshape(blocks * SLAB, W)
    dst_state_out = target_state[inverse].reshape(blocks * SLAB)
    return (sources.reshape(blocks * SLAB, W), dst_out, dst_state_out, relation)
```

```python
import jax
import jax.numpy as jnp
from jax import lax
from jax.experimental import pallas as pl
from jax.experimental.pallas import tpu as pltpu
from jax.sharding import Mesh, PartitionSpec as P

BATCH = 500
BATCHES = 2
NEG = 1000
SHIFT = 5
SLAB = 384
REL = 256
HALF = 128
W = 400
MID = 200
EP = 512
NP = 1024

ROW_RATE = 0.2
REL_RATE = 1.0

AXES = ("x", "zh", "y", "zl", "c")
PLANE = ("x", "y")
COLUMN = ("zh", "zl")
RIGHT = ("y", "zl", "c")

NN = (((1,), (0,)), ((), ()))
NT = (((1,), (1,)), ((), ()))
TN = (((0,), (0,)), ((), ()))


def parts(value):
    high = value.astype(jnp.bfloat16)
    low = (value - high.astype(jnp.float32)).astype(jnp.bfloat16)
    return (high, low)


def dot(first, second, dims):
    return lax.dot_general(first, second, dims, preferred_element_type=jnp.float32)


def dot3(first, second, dims):
    return (
        dot(first[0], second[0], dims) + dot(first[0], second[1], dims) + dot(first[1], second[0], dims)
    )


def pick(rows, ids):
    return (lax.broadcasted_iota(jnp.int32, (rows, EP), 0) == ids).astype(jnp.bfloat16)


def gather(table, hot):
    high, low = parts(table)
    return dot(high, hot, TN) + dot(low, hot, TN)


def scatter(hot, values):
    high, low = parts(values)
    return dot(hot, high, NT) + dot(hot, low, NT)


def column(row):
    return jnp.transpose(jnp.broadcast_to(row, (128, SLAB)))[:, :1]


def row(col):
    return jnp.transpose(jnp.broadcast_to(col, (SLAB, 128)))[:1, :]


def entity_update(table, state, grad):
    state = state + jnp.sum(grad * grad, axis=1, keepdims=True) * (1.0 / W)
    return (table - grad * (ROW_RATE / jnp.sqrt(state)), state)


def bucket(sources, relations, table, src_hot, dst_ids, rel_hot, src_ids, counts):
    s_re, s_im = (sources[:MID], sources[MID:])
    r_re, r_im = (relations[:MID], relations[MID:])
    queries = parts(jnp.concatenate([s_re * r_re - s_im * r_im, s_re * r_im + s_im * r_re], axis=0))
    rows = parts(table)
    logits = dot3(rows, queries, NN)
    tail = jnp.exp(-jnp.abs(logits))
    scale = jnp.where(src_ids >= 0, 1.0, 0.0) / (1.0 + tail)
    above = logits >= 0.0
    negative = jnp.where(above, 1.0, tail) * counts
    hit = lax.broadcasted_iota(jnp.int32, (SLAB, EP), 0) == dst_ids
    positive = jnp.where(hit, jnp.where(above, tail, 1.0), 0.0)
    weights = parts((negative - positive) * scale)
    grads = dot3(rows, weights, TN)
    g_re, g_im = (grads[:MID], grads[MID:])
    rho_grad = jnp.concatenate([g_re * s_re + g_im * s_im, g_im * s_re - g_re * s_im], axis=0)
    rel_grad = scatter(rel_hot, rho_grad)
    src_grad = jnp.concatenate([g_re * r_re + g_im * r_im, g_im * r_re - g_re * r_im], axis=0)
    src_grad = scatter(src_hot, src_grad)
    dst_grad = dot3(weights, queries, NT)
    return (rel_grad, src_grad, dst_grad)


def prepare_kernel(src_ref, rel_ref, ids_ref, neg_ref, sources_ref, relations_ref, counts_ref):
    sources_ref[...] = gather(src_ref[...], pick(SLAB, ids_ref[0:1, :]))
    relations_ref[...] = gather(rel_ref[...], pick(REL, ids_ref[4:5, :]))
    for batch in range(BATCHES):
        same = lax.broadcasted_iota(jnp.int32, (SLAB, NP), 0) == neg_ref[batch : batch + 1, :]
        total = jnp.sum(jnp.where(same, 1.0, 0.0), axis=1, keepdims=True)
        counts_ref[:, batch : batch + 1] = total * (1.0 / NEG)


def first_kernel(
    sources_ref, relations_ref, dst_ref, dst_state_ref, src_ref, src_state_ref, ids_ref, counts_ref,
    mine_ref, other_ref, src_out, src_state_out, dst_out, dst_state_out,
):
    rel_grad, src_grad, dst_grad = bucket(
        sources_ref[...], relations_ref[...], dst_ref[...], pick(SLAB, ids_ref[0:1, :]), ids_ref[2:3, :],
        pick(REL, ids_ref[5:6, :]), ids_ref[0:1, :], counts_ref[:, 0:1],
    )
    mine_ref[...] = rel_grad[:HALF]
    other_ref[...] = rel_grad[HALF:]
    src_out[...], src_state = entity_update(src_ref[...], column(src_state_ref[...]), src_grad)
    src_state_out[...] = row(src_state)
    dst_out[...], dst_state = entity_update(dst_ref[...], column(dst_state_ref[...]), dst_grad)
    dst_state_out[...] = row(dst_state)


def second_kernel(
    rel_mine_ref, rel_other_ref, dst_ref, dst_state_ref, src_ref, src_state_ref, ids_ref, counts_ref,
    mine_ref, other_ref, src_out, dst_out, dst_state_out,
):
    src_hot = pick(SLAB, ids_ref[1:2, :])
    rel_hot = pick(REL, ids_ref[6:7, :])
    relation = jnp.concatenate([rel_mine_ref[...], rel_other_ref[...]], axis=0)
    rel_grad, src_grad, dst_grad = bucket(
        gather(src_ref[...], src_hot), gather(relation, rel_hot), dst_ref[...], src_hot, ids_ref[3:4, :],
        rel_hot, ids_ref[1:2, :], counts_ref[:, 1:2],
    )
    mine_ref[...] = rel_grad[:HALF]
    other_ref[...] = rel_grad[HALF:]
    src_out[...], _ = entity_update(src_ref[...], column(src_state_ref[...]), src_grad)
    dst_out[...], dst_state = entity_update(dst_ref[...], column(dst_state_ref[...]), dst_grad)
    dst_state_out[...] = row(dst_state)


def call(kernel, outs, *args):
    shapes = [jax.ShapeDtypeStruct(shape, jnp.float32) for shape in outs]
    return pl.pallas_call(
        kernel,
        out_shape=shapes,
        in_specs=[pl.BlockSpec(memory_space=pltpu.VMEM)] * len(args),
        out_specs=[pl.BlockSpec(memory_space=pltpu.VMEM)] * len(shapes),
        compiler_params=pltpu.CompilerParams(vmem_limit_bytes=48 * 1024 * 1024),
    )(*args)


def shifted(value, steps):
    count = lax.axis_size(RIGHT)
    pairs = [(source, (source + steps) % count) for source in range(count)]
    return lax.ppermute(value, RIGHT, pairs)


def swapped(value):
    return lax.ppermute(value, "c", [(0, 1), (1, 0)])


def exchanged(value, axes):
    return lax.all_to_all(value, axes, split_axis=0, concat_axis=0, tiled=True)


def relation_update(mine, other, own, own_sums):
    lanes, layers = (lax.axis_size(PLANE), lax.axis_size(COLUMN))
    height = own.shape[0]
    half = mine + swapped(other)
    total = jnp.sum(exchanged(half.reshape(lanes, height, W), PLANE), axis=0)
    total = jnp.sum(exchanged(jnp.broadcast_to(total, (layers, height, W)), COLUMN), axis=0)
    own_sums = own_sums + total * total
    own = own - REL_RATE * total / jnp.sqrt(own_sums)
    half = exchanged(jnp.broadcast_to(own, (lanes, height, W)), PLANE).reshape(HALF, W)
    return (half, swapped(half), own, own_sums)


def padded(value, live, low):
    picked = value[low : low + BATCH]
    spot = lax.iota(jnp.int32, BATCH) + low
    return jnp.pad(jnp.where(spot < live, picked, -1), (0, EP - BATCH), constant_values=-1)


def body(
    src_embed, src_state, dst_embed, dst_state, relation, rel_state, edge_src, edge_dst, edge_rel, neg_rows, edge_count
):
    dst_table, dst_sums = (shifted(dst_embed, SHIFT), shifted(dst_state.reshape(1, SLAB), SHIFT))
    core = lax.axis_index("c")
    live = edge_count[0]
    near_rel = edge_rel[0] ^ (core * HALF)
    ids = jnp.stack(
        [
            padded(edge_src[0], live, 0),
            padded(edge_src[0], live, BATCH),
            padded(edge_dst[0], live, 0),
            padded(edge_dst[0], live, BATCH),
            padded(edge_rel[0], live, 0),
            padded(near_rel, live, 0),
            padded(near_rel, live, BATCH),
            jnp.full((EP,), -1, jnp.int32),
        ]
    )
    negs = jnp.pad(neg_rows[0], ((0, 0), (0, NP - NEG)), constant_values=-1)
    height = HALF // lax.axis_size(PLANE)
    start = core * HALF + lax.axis_index(PLANE) * height
    own = lax.dynamic_slice_in_dim(relation, start, height, 0)
    own_sums = lax.dynamic_slice_in_dim(rel_state, start, height, 0)
    src_sums = src_state.reshape(1, SLAB)

    sources, relations, counts = call(
        prepare_kernel, [(W, EP), (W, EP), (SLAB, BATCHES)], src_embed, relation, ids, negs
    )
    mine, other, src_table, src_sums, dst_table, dst_sums = call(
        first_kernel,
        [(HALF, W), (HALF, W), (SLAB, W), (1, SLAB), (SLAB, W), (1, SLAB)],
        sources, relations, dst_table, dst_sums, src_embed, src_sums, ids, counts,
    )
    near, far, own, own_sums = relation_update(mine, other, own, own_sums)
    mine, other, src_table, dst_table, dst_sums = call(
        second_kernel,
        [(HALF, W), (HALF, W), (SLAB, W), (SLAB, W), (1, SLAB)],
        near, far, dst_table, dst_sums, src_table, src_sums, ids, counts,
    )
    dst_table, dst_sums = (shifted(dst_table, -SHIFT), shifted(dst_sums, -SHIFT))
    near, far, own, own_sums = relation_update(mine, other, own, own_sums)
    first = core == 0
    relation = jnp.concatenate([jnp.where(first, near, far), jnp.where(first, far, near)], axis=0)
    return (src_table, dst_table, dst_sums.reshape(SLAB), relation)


def solution(mesh):
    left, right = (mesh.shape["left"], mesh.shape["right"])
    devices = mesh.devices.reshape(left // 2, 2, 4, right // 8, 2)
    inner = Mesh(devices, AXES)
    in_specs = (
        P(AXES, None),
        P(AXES),
        P(AXES, None),
        P(AXES),
        P(),
        P(),
        P(AXES, None),
        P(AXES, None),
        P(AXES, None),
        P(AXES, None, None),
        P(AXES),
    )
    out_specs = (P(AXES, None), P(AXES, None), P(AXES), P())
    return jax.shard_map(body, mesh=inner, in_specs=in_specs, out_specs=out_specs, check_vma=False)
```

```python
import jax
import jax.numpy as jnp
from jax import lax
from jax.experimental import pallas as pl
from jax.experimental.pallas import tpu as pltpu
from jax.sharding import Mesh, PartitionSpec as P

BATCH = 500
BATCHES = 2
NEG = 1000
SHIFT = 5
SLAB = 384
REL = 256
HALF = 128
W = 400
MID = 200
EP = 512
NP = 1024

ROW_RATE = 0.2
REL_RATE = 1.0

AXES = ("x", "zh", "y", "zl", "c")
PLANE = ("x", "y")
COLUMN = ("zh", "zl")
RIGHT = ("y", "zl", "c")

NN = (((1,), (0,)), ((), ()))
NT = (((1,), (1,)), ((), ()))
TN = (((0,), (0,)), ((), ()))


def parts(value):
    high = value.astype(jnp.bfloat16)
    low = (value - high.astype(jnp.float32)).astype(jnp.bfloat16)
    return (high, low)


def dot(first, second, dims):
    return lax.dot_general(first, second, dims, preferred_element_type=jnp.float32)


def dot3(first, second, dims):
    return (
        dot(first[0], second[0], dims) + dot(first[0], second[1], dims) + dot(first[1], second[0], dims)
    )


def pick(rows, ids):
    return (lax.broadcasted_iota(jnp.int32, (rows, EP), 0) == ids).astype(jnp.bfloat16)


def gather(table, hot):
    high, low = parts(table)
    return dot(high, hot, NN) + dot(low, hot, NN)


def scatter(values, hot):
    high, low = parts(values)
    return dot(high, hot, NT) + dot(low, hot, NT)


def entity_update(table, state, grad):
    state = state + jnp.sum(grad * grad, axis=0, keepdims=True) * (1.0 / W)
    return (table - grad * (ROW_RATE / jnp.sqrt(state)), state)


def bucket(sources, relations, table, src_hot, dst_ids, rel_hot, src_ids, counts):
    s_re, s_im = (sources[:MID], sources[MID:])
    r_re, r_im = (relations[:MID], relations[MID:])
    queries = parts(jnp.concatenate([s_re * r_re - s_im * r_im, s_re * r_im + s_im * r_re], axis=0))
    rows = parts(table)
    logits = dot3(rows, queries, TN)
    tail = jnp.exp(-jnp.abs(logits))
    scale = jnp.where(src_ids >= 0, 1.0, 0.0) / (1.0 + tail)
    above = logits >= 0.0
    negative = jnp.where(above, 1.0, tail) * counts
    hit = lax.broadcasted_iota(jnp.int32, (SLAB, EP), 0) == dst_ids
    positive = jnp.where(hit, jnp.where(above, tail, 1.0), 0.0)
    weights = parts((negative - positive) * scale)
    grads = dot3(rows, weights, NN)
    g_re, g_im = (grads[:MID], grads[MID:])
    rho_grad = jnp.concatenate([g_re * s_re + g_im * s_im, g_im * s_re - g_re * s_im], axis=0)
    rel_grad = scatter(rho_grad, rel_hot)
    src_grad = jnp.concatenate([g_re * r_re + g_im * r_im, g_im * r_re - g_re * r_im], axis=0)
    src_grad = scatter(src_grad, src_hot)
    dst_grad = dot3(queries, weights, NT)
    return (rel_grad, src_grad, dst_grad)


def put_halves(grad, mine_ref, other_ref):
    for ref, low in ((mine_ref, 0), (other_ref, HALF)):
        ref[:W, :] = grad[:, low : low + HALF]
        ref[W:, :] = jnp.zeros((EP - W, HALF), jnp.float32)


def prepare_kernel(
    place_ref, src_ref, rel_ref, rel_state_ref, ids_ref, neg_ref,
    sources_ref, relations_ref, counts_ref, own_ref, own_sums_ref, wide_ref,
):
    sources_ref[...] = gather(src_ref[...], pick(SLAB, ids_ref[0:1, :]))
    relations_ref[...] = gather(rel_ref[...], pick(REL, ids_ref[4:5, :]))
    for batch in range(BATCHES):
        same = lax.broadcasted_iota(jnp.int32, (SLAB, NP), 0) == neg_ref[batch : batch + 1, :]
        total = jnp.sum(jnp.where(same, 1.0, 0.0), axis=1, keepdims=True)
        counts_ref[:, batch : batch + 1] = total * (1.0 / NEG)
    height = own_ref.shape[0]
    wide_ref[W:, :] = jnp.ones((EP - W, HALF), jnp.float32)
    for source, target in ((rel_ref, own_ref), (rel_state_ref, own_sums_ref)):
        wide_ref[:W, :] = jnp.where(place_ref[0] == 0, source[:, :HALF], source[:, HALF:])
        target[...] = wide_ref[pl.ds(pl.multiple_of(place_ref[1] * height, height), height), :]


def first_kernel(
    sources_ref, relations_ref, dst_ref, dst_state_ref, src_ref, src_state_ref, ids_ref, counts_ref,
    mine_ref, other_ref, src_out, src_state_out, dst_out, dst_state_out,
):
    rel_grad, src_grad, dst_grad = bucket(
        sources_ref[...], relations_ref[...], dst_ref[...], pick(SLAB, ids_ref[0:1, :]), ids_ref[2:3, :],
        pick(REL, ids_ref[5:6, :]), ids_ref[0:1, :], counts_ref[:, 0:1],
    )
    put_halves(rel_grad, mine_ref, other_ref)
    src_out[...], src_state_out[...] = entity_update(src_ref[...], src_state_ref[...], src_grad)
    dst_out[...], dst_state_out[...] = entity_update(dst_ref[...], dst_state_ref[...], dst_grad)


def second_kernel(
    rel_mine_ref, rel_other_ref, dst_ref, dst_state_ref, src_ref, src_state_ref, ids_ref, counts_ref,
    mine_ref, other_ref, src_out, dst_out, dst_state_out,
):
    src_hot = pick(SLAB, ids_ref[1:2, :])
    rel_hot = pick(REL, ids_ref[6:7, :])
    relation = jnp.concatenate([rel_mine_ref[:W, :], rel_other_ref[:W, :]], axis=1)
    rel_grad, src_grad, dst_grad = bucket(
        gather(src_ref[...], src_hot), gather(relation, rel_hot), dst_ref[...], src_hot, ids_ref[3:4, :],
        rel_hot, ids_ref[1:2, :], counts_ref[:, 1:2],
    )
    put_halves(rel_grad, mine_ref, other_ref)
    src_out[...], _ = entity_update(src_ref[...], src_state_ref[...], src_grad)
    dst_out[...], dst_state_out[...] = entity_update(dst_ref[...], dst_state_ref[...], dst_grad)


def call(kernel, outs, *args, scalars=0, scratch=()):
    shapes = [jax.ShapeDtypeStruct(shape, jnp.float32) for shape in outs]
    vector = pl.BlockSpec(memory_space=pltpu.VMEM)
    scalar = pl.BlockSpec(memory_space=pltpu.SMEM)
    return pl.pallas_call(
        kernel,
        out_shape=shapes,
        in_specs=[scalar] * scalars + [vector] * (len(args) - scalars),
        out_specs=[vector] * len(shapes),
        scratch_shapes=scratch,
        compiler_params=pltpu.CompilerParams(vmem_limit_bytes=20 * 1024 * 1024),
    )(*args)


def shifted(value, steps):
    count = lax.axis_size(RIGHT)
    pairs = [(source, (source + steps) % count) for source in range(count)]
    return lax.ppermute(value, RIGHT, pairs)


def swapped(value):
    return lax.ppermute(value, "c", [(0, 1), (1, 0)])


def exchanged(value, axes):
    return lax.all_to_all(value, axes, split_axis=0, concat_axis=0, tiled=True)


def relation_update(mine, other, own, own_sums):
    lanes, layers = (lax.axis_size(PLANE), lax.axis_size(COLUMN))
    half = mine + swapped(other)
    total = jnp.sum(exchanged(half.reshape(lanes, *own.shape), PLANE), axis=0)
    total = jnp.sum(exchanged(jnp.broadcast_to(total, (layers, *own.shape)), COLUMN), axis=0)
    own_sums = own_sums + total * total
    own = own - REL_RATE * total / jnp.sqrt(own_sums)
    half = exchanged(jnp.broadcast_to(own, (lanes, *own.shape)), PLANE).reshape(EP, HALF)
    return (half, swapped(half), own, own_sums)


def padded(value, live, low):
    picked = value[low : low + BATCH]
    spot = lax.iota(jnp.int32, BATCH) + low
    return jnp.pad(jnp.where(spot < live, picked, -1), (0, EP - BATCH), constant_values=-1)


def body(
    src_embed, src_state, dst_embed, dst_state, relation, rel_state, edge_src, edge_dst, edge_rel, neg_rows, edge_count
):
    dst_table, dst_sums = (shifted(dst_embed.T, SHIFT), shifted(dst_state.reshape(1, SLAB), SHIFT))
    core = lax.axis_index("c")
    live = edge_count[0]
    near_rel = edge_rel[0] ^ (core * HALF)
    ids = jnp.stack(
        [
            padded(edge_src[0], live, 0),
            padded(edge_src[0], live, BATCH),
            padded(edge_dst[0], live, 0),
            padded(edge_dst[0], live, BATCH),
            padded(edge_rel[0], live, 0),
            padded(near_rel, live, 0),
            padded(near_rel, live, BATCH),
            jnp.full((EP,), -1, jnp.int32),
        ]
    )
    negs = jnp.pad(neg_rows[0], ((0, 0), (0, NP - NEG)), constant_values=-1)
    place = jnp.stack([core, lax.axis_index(PLANE)]).astype(jnp.int32)
    height = EP // lax.axis_size(PLANE)
    src_table, src_sums = (src_embed.T, src_state.reshape(1, SLAB))

    sources, relations, counts, own, own_sums = call(
        prepare_kernel,
        [(W, EP), (W, EP), (SLAB, BATCHES), (height, HALF), (height, HALF)],
        place, src_table, relation.T, rel_state.T, ids, negs,
        scalars=1,
        scratch=[pltpu.VMEM((EP, HALF), jnp.float32)],
    )
    mine, other, src_table, src_sums, dst_table, dst_sums = call(
        first_kernel,
        [(EP, HALF), (EP, HALF), (W, SLAB), (1, SLAB), (W, SLAB), (1, SLAB)],
        sources, relations, dst_table, dst_sums, src_table, src_sums, ids, counts,
    )
    near, far, own, own_sums = relation_update(mine, other, own, own_sums)
    mine, other, src_table, dst_table, dst_sums = call(
        second_kernel,
        [(EP, HALF), (EP, HALF), (W, SLAB), (W, SLAB), (1, SLAB)],
        near, far, dst_table, dst_sums, src_table, src_sums, ids, counts,
    )
    dst_table, dst_sums = (shifted(dst_table, -SHIFT), shifted(dst_sums, -SHIFT))
    near, far, own, own_sums = relation_update(mine, other, own, own_sums)
    first = core == 0
    relation = jnp.concatenate([jnp.where(first, near, far), jnp.where(first, far, near)], axis=1)
    return (src_table.T, dst_table.T, dst_sums.reshape(SLAB), relation[:W].T)


def solution(mesh):
    left, right = (mesh.shape["left"], mesh.shape["right"])
    devices = mesh.devices.reshape(left // 2, 2, 4, right // 8, 2)
    inner = Mesh(devices, AXES)
    in_specs = (
        P(AXES, None),
        P(AXES),
        P(AXES, None),
        P(AXES),
        P(),
        P(),
        P(AXES, None),
        P(AXES, None),
        P(AXES, None),
        P(AXES, None, None),
        P(AXES),
    )
    out_specs = (P(AXES, None), P(AXES, None), P(AXES), P())
    return jax.shard_map(body, mesh=inner, in_specs=in_specs, out_specs=out_specs, check_vma=False)
```

```python
import jax
import jax.numpy as jnp
from jax import lax
from jax.experimental import pallas as pl
from jax.experimental.pallas import tpu as pltpu
from jax.sharding import Mesh, PartitionSpec as P

BATCH = 500
BATCHES = 2
NEG = 1000
SHIFT = 5
SLAB = 384
REL = 256
HALF = 128
W = 400
MID = 200
EP = 512
NP = 1024

ROW_RATE = 0.2
REL_RATE = 1.0

AXES = ("x", "zh", "y", "zl", "c")
PLANE = ("x", "y")
COLUMN = ("zh", "zl")
RIGHT = ("y", "zl", "c")

NN = (((1,), (0,)), ((), ()))
NT = (((1,), (1,)), ((), ()))
TN = (((0,), (0,)), ((), ()))


def parts(value):
    high = value.astype(jnp.bfloat16)
    low = (value - high.astype(jnp.float32)).astype(jnp.bfloat16)
    return (high, low)


def dot(first, second, dims):
    return lax.dot_general(first, second, dims, preferred_element_type=jnp.float32)


def dot3(first, second, dims):
    return (
        dot(first[0], second[0], dims) + dot(first[0], second[1], dims) + dot(first[1], second[0], dims)
    )


def pick(rows, ids):
    return (lax.broadcasted_iota(jnp.int32, (rows, EP), 0) == ids).astype(jnp.bfloat16)


def gather(table, hot):
    high, low = parts(table)
    return dot(high, hot, NN) + dot(low, hot, NN)


def scatter(values, hot):
    high, low = parts(values)
    return dot(high, hot, NT) + dot(low, hot, NT)


def entity_update(table, state, grad):
    state = state + jnp.sum(grad * grad, axis=0, keepdims=True) * (1.0 / W)
    return (table - grad * (ROW_RATE / jnp.sqrt(state)), state)


def query(sources, relations):
    s_re, s_im = (sources[:MID], sources[MID:])
    r_re, r_im = (relations[:MID], relations[MID:])
    return parts(jnp.concatenate([s_re * r_re - s_im * r_im, s_re * r_im + s_im * r_re], axis=0))


def against(grads, other):
    g_re, g_im = (grads[:MID], grads[MID:])
    o_re, o_im = (other[:MID], other[MID:])
    return jnp.concatenate([g_re * o_re + g_im * o_im, g_im * o_re - g_re * o_im], axis=0)


def edge_weights(logits, src_ids, dst_ids, counts):
    tail = jnp.exp(-jnp.abs(logits))
    scale = jnp.where(src_ids >= 0, 1.0, 0.0) / (1.0 + tail)
    above = logits >= 0.0
    negative = jnp.where(above, 1.0, tail) * counts
    hit = lax.broadcasted_iota(jnp.int32, (SLAB, EP), 0) == dst_ids
    positive = jnp.where(hit, jnp.where(above, tail, 1.0), 0.0)
    return parts((negative - positive) * scale)


def put(refs, values):
    for ref, value in zip(refs, values, strict=True):
        ref[...] = value


def relation_side(batch, queries, sources, relations, dst_ref, ids_ref, counts_ref, mine_ref, other_ref, weight_refs, way_ref):
    rows = parts(dst_ref[...])
    src_ids, dst_ids = (ids_ref[batch : batch + 1, :], ids_ref[2 + batch : 3 + batch, :])
    weights = edge_weights(dot3(rows, queries, TN), src_ids, dst_ids, counts_ref[:, batch : batch + 1])
    grads = dot3(rows, weights, NN)
    rel_grad = scatter(against(grads, sources), pick(REL, ids_ref[5 + batch : 6 + batch, :]))
    for ref, low in ((mine_ref, 0), (other_ref, HALF)):
        ref[:W, :] = rel_grad[:, low : low + HALF]
        ref[W:, :] = jnp.zeros((EP - W, HALF), jnp.float32)
    put(weight_refs, weights)
    way_ref[...] = against(grads, relations)


def prepare_kernel(
    place_ref, src_ref, rel_ref, rel_state_ref, ids_ref, neg_ref, dst_state_ref,
    sources_ref, relations_ref, high_ref, low_ref, counts_ref, own_ref, own_sums_ref, dst_state_out, wide_ref,
):
    sources = gather(src_ref[...], pick(SLAB, ids_ref[0:1, :]))
    relations = gather(rel_ref[...], pick(REL, ids_ref[4:5, :]))
    put((sources_ref, relations_ref), (sources, relations))
    put((high_ref, low_ref), query(sources, relations))
    for batch in range(BATCHES):
        same = lax.broadcasted_iota(jnp.int32, (SLAB, NP), 0) == neg_ref[batch : batch + 1, :]
        total = jnp.sum(jnp.where(same, 1.0, 0.0), axis=1, keepdims=True)
        counts_ref[:, batch : batch + 1] = total * (1.0 / NEG)
    height = own_ref.shape[0]
    wide_ref[W:, :] = jnp.ones((EP - W, HALF), jnp.float32)
    for source, target in ((rel_ref, own_ref), (rel_state_ref, own_sums_ref)):
        wide_ref[:W, :] = jnp.where(place_ref[0] == 0, source[:, :HALF], source[:, HALF:])
        target[...] = wide_ref[pl.ds(pl.multiple_of(place_ref[1] * height, height), height), :]
    dst_state_out[...] = dst_state_ref[...]


def first_relation_kernel(
    sources_ref, relations_ref, high_ref, low_ref, dst_ref, ids_ref, counts_ref,
    mine_ref, other_ref, weight_high_ref, weight_low_ref, way_ref,
):
    relation_side(
        0, (high_ref[...], low_ref[...]), sources_ref[...], relations_ref[...], dst_ref, ids_ref, counts_ref,
        mine_ref, other_ref, (weight_high_ref, weight_low_ref), way_ref,
    )


def first_entity_kernel(
    high_ref, low_ref, weight_high_ref, weight_low_ref, way_ref, dst_ref, dst_state_ref, src_ref, src_state_ref, ids_ref,
    src_out, src_state_out, dst_out, dst_state_out, sources_ref,
):
    src_grad = scatter(way_ref[...], pick(SLAB, ids_ref[0:1, :]))
    src_table, src_state_out[...] = entity_update(src_ref[...], src_state_ref[...], src_grad)
    src_out[...] = src_table
    sources_ref[...] = gather(src_table, pick(SLAB, ids_ref[1:2, :]))
    dst_grad = dot3((high_ref[...], low_ref[...]), (weight_high_ref[...], weight_low_ref[...]), NT)
    dst_out[...], dst_state_out[...] = entity_update(dst_ref[...], dst_state_ref[...], dst_grad)


def second_relation_kernel(
    rel_mine_ref, rel_other_ref, sources_ref, dst_ref, ids_ref, counts_ref,
    mine_ref, other_ref, high_ref, low_ref, weight_high_ref, weight_low_ref, way_ref,
):
    relation = jnp.concatenate([rel_mine_ref[:W, :], rel_other_ref[:W, :]], axis=1)
    sources, relations = (sources_ref[...], gather(relation, pick(REL, ids_ref[6:7, :])))
    queries = query(sources, relations)
    put((high_ref, low_ref), queries)
    relation_side(
        1, queries, sources, relations, dst_ref, ids_ref, counts_ref,
        mine_ref, other_ref, (weight_high_ref, weight_low_ref), way_ref,
    )


def second_target_kernel(high_ref, low_ref, weight_high_ref, weight_low_ref, dst_ref, dst_state_ref, out_ref):
    dst_grad = dot3((high_ref[...], low_ref[...]), (weight_high_ref[...], weight_low_ref[...]), NT)
    out_ref[:W, :], state = entity_update(dst_ref[...], dst_state_ref[...], dst_grad)
    out_ref[W:, :] = jnp.broadcast_to(state, (8, SLAB))


def second_source_kernel(way_ref, src_ref, src_state_ref, ids_ref, src_out):
    src_grad = scatter(way_ref[...], pick(SLAB, ids_ref[1:2, :]))
    src_out[...], _ = entity_update(src_ref[...], src_state_ref[...], src_grad)


def call(kernel, outs, *args, scalars=0, scratch=(), passes=0):
    shapes = [shape if isinstance(shape, jax.ShapeDtypeStruct) else jax.ShapeDtypeStruct(shape, jnp.float32) for shape in outs]
    vector = pl.BlockSpec(memory_space=pltpu.VMEM)
    scalar = pl.BlockSpec(memory_space=pltpu.SMEM)
    moved = sum(value.size * value.dtype.itemsize for value in (*args, *shapes))
    return pl.pallas_call(
        kernel,
        out_shape=shapes,
        in_specs=[scalar] * scalars + [vector] * (len(args) - scalars),
        out_specs=[vector] * len(shapes),
        scratch_shapes=scratch,
        cost_estimate=pl.CostEstimate(flops=passes * 2 * EP * EP * SLAB, bytes_accessed=moved, transcendentals=0),
        compiler_params=pltpu.CompilerParams(vmem_limit_bytes=20 * 1024 * 1024),
    )(*args)


def shifted(value, steps):
    count = lax.axis_size(RIGHT)
    pairs = [(source, (source + steps) % count) for source in range(count)]
    return lax.ppermute(value, RIGHT, pairs)


def swapped(value):
    return lax.ppermute(value, "c", [(0, 1), (1, 0)])


def exchanged(value, axes):
    return lax.all_to_all(value, axes, split_axis=0, concat_axis=0, tiled=True)


def relation_update(mine, other, own, own_sums, beside=None):
    lanes, layers = (lax.axis_size(PLANE), lax.axis_size(COLUMN))
    half = mine + swapped(other)
    total = jnp.sum(exchanged(half.reshape(lanes, *own.shape), PLANE), axis=0)
    total = jnp.sum(exchanged(jnp.broadcast_to(total, (layers, *own.shape)), COLUMN), axis=0)
    own_sums = own_sums + total * total
    own = own - REL_RATE * total / jnp.sqrt(own_sums)
    if beside is not None:
        own, beside = lax.optimization_barrier((own, beside))
    half = exchanged(jnp.broadcast_to(own, (lanes, *own.shape)), PLANE).reshape(EP, HALF)
    return (half, swapped(half), own, own_sums, beside)


def padded(value, live, low):
    picked = value[low : low + BATCH]
    spot = lax.iota(jnp.int32, BATCH) + low
    return jnp.pad(jnp.where(spot < live, picked, -1), (0, EP - BATCH), constant_values=-1)


def body(
    src_embed, src_state, dst_embed, dst_state, relation, rel_state, edge_src, edge_dst, edge_rel, neg_rows, edge_count
):
    dst_table = shifted(dst_embed.T, SHIFT)
    core = lax.axis_index("c")
    live = edge_count[0]
    near_rel = edge_rel[0] ^ (core * HALF)
    ids = jnp.stack(
        [
            padded(edge_src[0], live, 0),
            padded(edge_src[0], live, BATCH),
            padded(edge_dst[0], live, 0),
            padded(edge_dst[0], live, BATCH),
            padded(edge_rel[0], live, 0),
            padded(near_rel, live, 0),
            padded(near_rel, live, BATCH),
            jnp.full((EP,), -1, jnp.int32),
        ]
    )
    negs = jnp.pad(neg_rows[0], ((0, 0), (0, NP - NEG)), constant_values=-1)
    place = jnp.stack([core, lax.axis_index(PLANE)]).astype(jnp.int32)
    height = EP // lax.axis_size(PLANE)
    src_table, src_sums = (src_embed.T, src_state.reshape(1, SLAB))

    high, low = [jax.ShapeDtypeStruct((W, EP), jnp.bfloat16)] * 2
    weight_high, weight_low = [jax.ShapeDtypeStruct((SLAB, EP), jnp.bfloat16)] * 2
    halves = [(EP, HALF), (EP, HALF)]
    flat = (1, SLAB)

    sources, relations, *queries, counts, own, own_sums, dst_sums = call(
        prepare_kernel,
        [(W, EP), (W, EP), high, low, (SLAB, BATCHES), (height, HALF), (height, HALF), flat],
        place, src_table, relation.T, rel_state.T, ids, negs, dst_state.reshape(flat),
        scalars=1, scratch=[pltpu.VMEM((EP, HALF), jnp.float32)], passes=4,
    )
    dst_table, dst_sums = lax.optimization_barrier((dst_table, shifted(dst_sums, SHIFT)))
    mine, other, *weights, way = call(
        first_relation_kernel,
        [*halves, weight_high, weight_low, (W, EP)],
        sources, relations, *queries, dst_table, ids, counts, passes=8,
    )
    near, far, own, own_sums, _ = relation_update(mine, other, own, own_sums)
    src_table, src_sums, dst_table, dst_sums, sources = call(
        first_entity_kernel,
        [(W, SLAB), flat, (W, SLAB), flat, (W, EP)],
        *queries, *weights, way, dst_table, dst_sums, src_table, src_sums, ids, passes=7,
    )
    mine, other, high, low, weight_high, weight_low, way = call(
        second_relation_kernel,
        [*halves, high, low, weight_high, weight_low, (W, EP)],
        near, far, sources, dst_table, ids, counts, passes=10,
    )
    (home,) = call(second_target_kernel, [(W + 8, SLAB)], high, low, weight_high, weight_low, dst_table, dst_sums, passes=3)
    home = shifted(home, -SHIFT)
    (src_table,) = call(second_source_kernel, [(W, SLAB)], way, src_table, src_sums, ids, passes=2)
    near, far, own, own_sums, home = relation_update(mine, other, own, own_sums, home)
    first = core == 0
    relation = jnp.concatenate([jnp.where(first, near, far), jnp.where(first, far, near)], axis=1)
    return (src_table.T, home[:W].T, home[W], relation[:W].T)


def solution(mesh):
    left, right = (mesh.shape["left"], mesh.shape["right"])
    devices = mesh.devices.reshape(left // 2, 2, 4, right // 8, 2)
    inner = Mesh(devices, AXES)
    in_specs = (
        P(AXES, None),
        P(AXES),
        P(AXES, None),
        P(AXES),
        P(),
        P(),
        P(AXES, None),
        P(AXES, None),
        P(AXES, None),
        P(AXES, None, None),
        P(AXES),
    )
    out_specs = (P(AXES, None), P(AXES, None), P(AXES), P())
    return jax.shard_map(body, mesh=inner, in_specs=in_specs, out_specs=out_specs, check_vma=False)
```

```python
import jax
import jax.numpy as jnp
from jax import lax
from jax.experimental import pallas as pl
from jax.experimental.pallas import tpu as pltpu
from jax.sharding import Mesh, PartitionSpec as P

BATCH = 500
BATCHES = 2
NEG = 1000
SHIFT = 5
SLAB = 384
REL = 256
HALF = 128
W = 400
MID = 200
EP = 512
NP = 1024
CUT = 200

ROW_RATE = 0.2
REL_RATE = 1.0

AXES = ("x", "zh", "y", "zl", "c")
PLANE = ("x", "y")
COLUMN = ("zh", "zl")
RIGHT = ("y", "zl", "c")

NN = (((1,), (0,)), ((), ()))
NT = (((1,), (1,)), ((), ()))
TN = (((0,), (0,)), ((), ()))


def parts(value):
    high = value.astype(jnp.bfloat16)
    low = (value - high.astype(jnp.float32)).astype(jnp.bfloat16)
    return (high, low)


def dot(first, second, dims):
    return lax.dot_general(first, second, dims, preferred_element_type=jnp.float32)


def dot3(first, second, dims):
    return (
        dot(first[0], second[0], dims) + dot(first[0], second[1], dims) + dot(first[1], second[0], dims)
    )


def pick(rows, ids):
    return (lax.broadcasted_iota(jnp.int32, (rows, EP), 0) == ids).astype(jnp.bfloat16)


def gather(table, hot):
    high, low = parts(table)
    return dot(high, hot, NN) + dot(low, hot, NN)


def scatter(values, hot):
    high, low = parts(values)
    return dot(high, hot, NT) + dot(low, hot, NT)


def entity_update(table, state, grad):
    state = state + jnp.sum(grad * grad, axis=0, keepdims=True) * (1.0 / W)
    return (table - grad * (ROW_RATE / jnp.sqrt(state)), state)


def query(sources, relations):
    s_re, s_im = (sources[:MID], sources[MID:])
    r_re, r_im = (relations[:MID], relations[MID:])
    return parts(jnp.concatenate([s_re * r_re - s_im * r_im, s_re * r_im + s_im * r_re], axis=0))


def against(grads, other):
    g_re, g_im = (grads[:MID], grads[MID:])
    o_re, o_im = (other[:MID], other[MID:])
    return jnp.concatenate([g_re * o_re + g_im * o_im, g_im * o_re - g_re * o_im], axis=0)


def edge_weights(logits, src_ids, dst_ids, counts):
    tail = jnp.exp(-jnp.abs(logits))
    scale = jnp.where(src_ids >= 0, 1.0, 0.0) / (1.0 + tail)
    above = logits >= 0.0
    negative = jnp.where(above, 1.0, tail) * counts
    hit = lax.broadcasted_iota(jnp.int32, (SLAB, EP), 0) == dst_ids
    positive = jnp.where(hit, jnp.where(above, tail, 1.0), 0.0)
    return parts((negative - positive) * scale)


def put(refs, values):
    for ref, value in zip(refs, values, strict=True):
        ref[...] = value


def bucket(batch, sources, relations, dst_ref, ids_ref, counts_ref, mine_ref, other_ref):
    queries, rows = (query(sources, relations), parts(dst_ref[...]))
    src_ids, dst_ids = (ids_ref[batch : batch + 1, :], ids_ref[2 + batch : 3 + batch, :])
    weights = edge_weights(dot3(rows, queries, TN), src_ids, dst_ids, counts_ref[:, batch : batch + 1])
    grads = dot3(rows, weights, NN)
    rel_grad = scatter(against(grads, sources), pick(REL, ids_ref[5 + batch : 6 + batch, :]))
    for ref, low in ((mine_ref, 0), (other_ref, HALF)):
        ref[:W, :] = rel_grad[:, low : low + HALF]
        ref[W:, :] = jnp.zeros((EP - W, HALF), jnp.float32)
    src_grad = scatter(against(grads, relations), pick(SLAB, src_ids))
    return (src_grad, dot3(queries, weights, NT))


def prepare_kernel(
    place_ref, src_ref, rel_ref, rel_state_ref, ids_ref, neg_ref, dst_state_ref,
    sources_ref, relations_ref, counts_ref, own_ref, own_sums_ref, dst_state_out, wide_ref,
):
    sources_ref[...] = gather(src_ref[...], pick(SLAB, ids_ref[0:1, :]))
    relations_ref[...] = gather(rel_ref[...], pick(REL, ids_ref[4:5, :]))
    for batch in range(BATCHES):
        same = lax.broadcasted_iota(jnp.int32, (SLAB, NP), 0) == neg_ref[batch : batch + 1, :]
        total = jnp.sum(jnp.where(same, 1.0, 0.0), axis=1, keepdims=True)
        counts_ref[:, batch : batch + 1] = total * (1.0 / NEG)
    height = own_ref.shape[0]
    wide_ref[W:, :] = jnp.ones((EP - W, HALF), jnp.float32)
    for source, target in ((rel_ref, own_ref), (rel_state_ref, own_sums_ref)):
        wide_ref[:W, :] = jnp.where(place_ref[0] == 0, source[:, :HALF], source[:, HALF:])
        target[...] = wide_ref[pl.ds(pl.multiple_of(place_ref[1] * height, height), height), :]
    dst_state_out[...] = dst_state_ref[...]


def first_kernel(
    sources_ref, relations_ref, dst_ref, dst_state_ref, src_ref, src_state_ref, ids_ref, counts_ref,
    mine_ref, other_ref, src_out, src_state_out, dst_out, dst_state_out,
):
    src_grad, dst_grad = bucket(
        0, sources_ref[...], relations_ref[...], dst_ref, ids_ref, counts_ref, mine_ref, other_ref
    )
    src_out[...], src_state_out[...] = entity_update(src_ref[...], src_state_ref[...], src_grad)
    dst_out[...], dst_state_out[...] = entity_update(dst_ref[...], dst_state_ref[...], dst_grad)


def second_kernel(
    rel_mine_ref, rel_other_ref, dst_ref, dst_state_ref, src_ref, src_state_ref, ids_ref, counts_ref,
    mine_ref, other_ref, src_out, upper_out, lower_out,
):
    relation = jnp.concatenate([rel_mine_ref[:W, :], rel_other_ref[:W, :]], axis=1)
    sources = gather(src_ref[...], pick(SLAB, ids_ref[1:2, :]))
    relations = gather(relation, pick(REL, ids_ref[6:7, :]))
    src_grad, dst_grad = bucket(1, sources, relations, dst_ref, ids_ref, counts_ref, mine_ref, other_ref)
    dst_table, dst_state = entity_update(dst_ref[...], dst_state_ref[...], dst_grad)
    upper_out[...] = dst_table[:CUT]
    lower_out[: W - CUT, :] = dst_table[CUT:]
    lower_out[W - CUT :, :] = jnp.broadcast_to(dst_state, (8, SLAB))
    src_out[...], _ = entity_update(src_ref[...], src_state_ref[...], src_grad)


def call(kernel, outs, *args, scalars=0, scratch=(), passes=0):
    shapes = [shape if isinstance(shape, jax.ShapeDtypeStruct) else jax.ShapeDtypeStruct(shape, jnp.float32) for shape in outs]
    vector = pl.BlockSpec(memory_space=pltpu.VMEM)
    scalar = pl.BlockSpec(memory_space=pltpu.SMEM)
    moved = sum(value.size * value.dtype.itemsize for value in (*args, *shapes))
    return pl.pallas_call(
        kernel,
        out_shape=shapes,
        in_specs=[scalar] * scalars + [vector] * (len(args) - scalars),
        out_specs=[vector] * len(shapes),
        scratch_shapes=scratch,
        cost_estimate=pl.CostEstimate(flops=passes * 2 * EP * EP * SLAB, bytes_accessed=moved, transcendentals=0),
        compiler_params=pltpu.CompilerParams(vmem_limit_bytes=16 * 1024 * 1024),
    )(*args)


def shifted(value, steps):
    count = lax.axis_size(RIGHT)
    pairs = [(source, (source + steps) % count) for source in range(count)]
    return lax.ppermute(value, RIGHT, pairs)


def swapped(value):
    return lax.ppermute(value, "c", [(0, 1), (1, 0)])


def exchanged(value, axes):
    return lax.all_to_all(value, axes, split_axis=0, concat_axis=0, tiled=True)


def relation_update(mine, other, own, own_sums, upper=None, lower=None):
    lanes, layers = (lax.axis_size(PLANE), lax.axis_size(COLUMN))
    half = mine + swapped(other)
    total = jnp.sum(exchanged(half.reshape(lanes, *own.shape), PLANE), axis=0)
    if upper is not None:
        total, upper = lax.optimization_barrier((total, shifted(upper, -SHIFT)))
    total = jnp.sum(exchanged(jnp.broadcast_to(total, (layers, *own.shape)), COLUMN), axis=0)
    if lower is not None:
        total, lower = lax.optimization_barrier((total, lower))
        lower = shifted(lower, -SHIFT)
    own_sums = own_sums + total * total
    own = own - REL_RATE * total / jnp.sqrt(own_sums)
    half = exchanged(jnp.broadcast_to(own, (lanes, *own.shape)), PLANE).reshape(EP, HALF)
    return (half, swapped(half), own, own_sums, upper, lower)


def padded(value, live, low):
    picked = value[low : low + BATCH]
    spot = lax.iota(jnp.int32, BATCH) + low
    return jnp.pad(jnp.where(spot < live, picked, -1), (0, EP - BATCH), constant_values=-1)


def body(
    src_embed, src_state, dst_embed, dst_state, relation, rel_state, edge_src, edge_dst, edge_rel, neg_rows, edge_count
):
    dst_table = shifted(dst_embed.T, SHIFT)
    core = lax.axis_index("c")
    live = edge_count[0]
    near_rel = edge_rel[0] ^ (core * HALF)
    ids = jnp.stack(
        [
            padded(edge_src[0], live, 0),
            padded(edge_src[0], live, BATCH),
            padded(edge_dst[0], live, 0),
            padded(edge_dst[0], live, BATCH),
            padded(edge_rel[0], live, 0),
            padded(near_rel, live, 0),
            padded(near_rel, live, BATCH),
            jnp.full((EP,), -1, jnp.int32),
        ]
    )
    negs = jnp.pad(neg_rows[0], ((0, 0), (0, NP - NEG)), constant_values=-1)
    place = jnp.stack([core, lax.axis_index(PLANE)]).astype(jnp.int32)
    height = EP // lax.axis_size(PLANE)
    src_table, src_sums = (src_embed.T, src_state.reshape(1, SLAB))

    flat = (1, SLAB)
    sources, relations, counts, own, own_sums, dst_sums = call(
        prepare_kernel,
        [(W, EP), (W, EP), (SLAB, BATCHES), (height, HALF), (height, HALF), flat],
        place, src_table, relation.T, rel_state.T, ids, negs, dst_state.reshape(flat),
        scalars=1, scratch=[pltpu.VMEM((EP, HALF), jnp.float32)], passes=4,
    )
    dst_table, dst_sums = lax.optimization_barrier((dst_table, shifted(dst_sums, SHIFT)))
    mine, other, src_table, src_sums, dst_table, dst_sums = call(
        first_kernel,
        [(EP, HALF), (EP, HALF), (W, SLAB), flat, (W, SLAB), flat],
        sources, relations, dst_table, dst_sums, src_table, src_sums, ids, counts, passes=13,
    )
    near, far, own, own_sums, _, _ = relation_update(mine, other, own, own_sums)
    mine, other, src_table, upper, lower = call(
        second_kernel,
        [(EP, HALF), (EP, HALF), (W, SLAB), (CUT, SLAB), (W + 8 - CUT, SLAB)],
        near, far, dst_table, dst_sums, src_table, src_sums, ids, counts, passes=17,
    )
    near, far, own, own_sums, upper, lower = relation_update(mine, other, own, own_sums, upper, lower)
    first = core == 0
    relation = jnp.concatenate([jnp.where(first, near, far), jnp.where(first, far, near)], axis=1)
    dst_table = jnp.concatenate([upper, lower[: W - CUT]], axis=0)
    return (src_table.T, dst_table.T, lower[W - CUT], relation[:W].T)


def solution(mesh):
    left, right = (mesh.shape["left"], mesh.shape["right"])
    devices = mesh.devices.reshape(left // 2, 2, 4, right // 8, 2)
    inner = Mesh(devices, AXES)
    in_specs = (
        P(AXES, None),
        P(AXES),
        P(AXES, None),
        P(AXES),
        P(),
        P(),
        P(AXES, None),
        P(AXES, None),
        P(AXES, None),
        P(AXES, None, None),
        P(AXES),
    )
    out_specs = (P(AXES, None), P(AXES, None), P(AXES), P())
    return jax.shard_map(body, mesh=inner, in_specs=in_specs, out_specs=out_specs, check_vma=False)
```

```python
import jax
import jax.numpy as jnp
from jax import lax
from jax.experimental import pallas as pl
from jax.experimental.pallas import tpu as pltpu
from jax.sharding import Mesh, PartitionSpec as P

BATCH = 500
BATCHES = 2
NEG = 1000
SHIFT = 5
SLAB = 384
REL = 256
HALF = 128
W = 400
MID = 200
EP = 512
NP = 1024
CUT = 200

ROW_RATE = 0.2
REL_RATE = 1.0

AXES = ("x", "zh", "y", "zl", "c")
PLANE = ("x", "y")
COLUMN = ("zh", "zl")
RIGHT = ("y", "zl", "c")

NN = (((1,), (0,)), ((), ()))
NT = (((1,), (1,)), ((), ()))
TN = (((0,), (0,)), ((), ()))


def parts(value):
    high = value.astype(jnp.bfloat16)
    low = (value - high.astype(jnp.float32)).astype(jnp.bfloat16)
    return (high, low)


def dot(first, second, dims):
    return lax.dot_general(first, second, dims, preferred_element_type=jnp.float32)


def joined(values, axis):
    return jnp.concatenate(values, axis=axis)


def dot3(first, second, dims):
    (one,), (two,) = dims[0]
    return dot(joined([first[0], first[0], first[1]], one), joined([second[0], second[1], second[0]], two), dims)


def pick(rows, ids):
    return (lax.broadcasted_iota(jnp.int32, (rows, EP), 0) == ids).astype(jnp.bfloat16)


def gather(table, hot):
    return dot(joined(parts(table), 1), joined([hot, hot], 0), NN)


def scatter(values, hot):
    high, low = parts(values)
    return dot(high, hot, NT) + dot(low, hot, NT)


def entity_update(table, state, grad):
    state = state + jnp.sum(grad * grad, axis=0, keepdims=True) * (1.0 / W)
    return (table - grad * (ROW_RATE / jnp.sqrt(state)), state)


def query(sources, relations):
    s_re, s_im = (sources[:MID], sources[MID:])
    r_re, r_im = (relations[:MID], relations[MID:])
    return parts(jnp.concatenate([s_re * r_re - s_im * r_im, s_re * r_im + s_im * r_re], axis=0))


def against(grads, other):
    g_re, g_im = (grads[:MID], grads[MID:])
    o_re, o_im = (other[:MID], other[MID:])
    return jnp.concatenate([g_re * o_re + g_im * o_im, g_im * o_re - g_re * o_im], axis=0)


def edge_weights(logits, dst_ids, counts):
    hit = lax.broadcasted_iota(jnp.int32, (SLAB, EP), 0) == dst_ids
    positive = jnp.where(hit, 0.5, 0.0)
    return parts((counts - positive) + (counts + positive) * jnp.tanh(0.5 * logits))


def put(refs, values):
    for ref, value in zip(refs, values, strict=True):
        ref[...] = value


def put(refs, values):
    for ref, value in zip(refs, values, strict=True):
        ref[...] = value


def relation_side(batch, sources, relations, dst_ref, ids_ref, counts_ref, mine_ref, other_ref, way_ref, query_refs, weight_refs):
    queries, rows = (query(sources, relations), parts(dst_ref[...]))
    put(query_refs, queries)
    dst_ids = ids_ref[2 + batch : 3 + batch, :]
    weights = edge_weights(dot3(rows, queries, TN), dst_ids, counts_ref[:, batch : batch + 1])
    put(weight_refs, weights)
    grads = dot3(rows, weights, NN)
    rel_grad = scatter(against(grads, sources), pick(REL, ids_ref[5 + batch : 6 + batch, :]))
    put((mine_ref, other_ref), (rel_grad[:, :HALF], rel_grad[:, HALF:]))
    way_ref[...] = against(grads, relations)


def target_update(query_refs, weight_refs, dst_ref, dst_state_ref):
    queries, weights = [tuple(ref[...] for ref in refs) for refs in (query_refs, weight_refs)]
    return entity_update(dst_ref[...], dst_state_ref[...], dot3(queries, weights, NT))


def source_update(batch, way_ref, src_ref, src_state_ref, ids_ref):
    src_grad = scatter(way_ref[...], pick(SLAB, ids_ref[batch : batch + 1, :]))
    return entity_update(src_ref[...], src_state_ref[...], src_grad)


def prepare_kernel(
    place_ref, src_ref, rel_ref, rel_state_ref, ids_ref, neg_ref, dst_state_ref,
    sources_ref, relations_ref, counts_ref, own_ref, own_sums_ref, dst_state_out,
):
    sources_ref[...] = gather(src_ref[...], pick(SLAB, ids_ref[0:1, :]))
    relations_ref[...] = gather(rel_ref[...], pick(REL, ids_ref[4:5, :]))
    for batch in range(BATCHES):
        same = lax.broadcasted_iota(jnp.int32, (SLAB, NP), 0) == neg_ref[batch : batch + 1, :]
        total = jnp.sum(jnp.where(same, 1.0, 0.0), axis=1, keepdims=True)
        counts_ref[:, batch : batch + 1] = total * (0.5 / NEG)
    for source, target in ((rel_ref, own_ref), (rel_state_ref, own_sums_ref)):
        target[...] = jnp.where(place_ref[0] == 0, source[:, :HALF], source[:, HALF:])
    dst_state_out[...] = dst_state_ref[...]


def first_relation_kernel(sources_ref, relations_ref, dst_ref, ids_ref, counts_ref, mine_ref, other_ref, way_ref, *kept):
    relation_side(
        0, sources_ref[...], relations_ref[...], dst_ref, ids_ref, counts_ref, mine_ref, other_ref, way_ref, kept[:2], kept[2:]
    )


def first_entity_kernel(
    way_ref, high_ref, low_ref, weight_high_ref, weight_low_ref, dst_ref, dst_state_ref, src_ref, src_state_ref, ids_ref,
    src_out, src_state_out, dst_out, dst_state_out,
):
    src_out[...], src_state_out[...] = source_update(0, way_ref, src_ref, src_state_ref, ids_ref)
    dst_out[...], dst_state_out[...] = target_update(
        (high_ref, low_ref), (weight_high_ref, weight_low_ref), dst_ref, dst_state_ref
    )


def gather_kernel(src_ref, ids_ref, sources_ref):
    sources_ref[...] = gather(src_ref[...], pick(SLAB, ids_ref[1:2, :]))


def second_relation_kernel(
    rel_mine_ref, rel_other_ref, sources_ref, dst_ref, ids_ref, counts_ref, mine_ref, other_ref, way_ref, *kept
):
    relation = jnp.concatenate([rel_mine_ref[...], rel_other_ref[...]], axis=1)
    relations = gather(relation, pick(REL, ids_ref[6:7, :]))
    relation_side(
        1, sources_ref[...], relations, dst_ref, ids_ref, counts_ref, mine_ref, other_ref, way_ref, kept[:2], kept[2:]
    )


def second_target_kernel(
    high_ref, low_ref, weight_high_ref, weight_low_ref, dst_ref, dst_state_ref, upper_out, lower_out
):
    dst_table, dst_state = target_update((high_ref, low_ref), (weight_high_ref, weight_low_ref), dst_ref, dst_state_ref)
    upper_out[...] = dst_table[:CUT]
    lower_out[: W - CUT, :] = dst_table[CUT:]
    lower_out[W - CUT :, :] = jnp.broadcast_to(dst_state, (8, SLAB))


def last_kernel(
    way_ref, src_ref, src_state_ref, ids_ref, upper_ref, lower_ref, src_out, dst_out, dst_state_out, sem
):
    copies = [
        pltpu.make_async_copy(upper_ref, dst_out.at[pl.ds(0, CUT)], sem.at[0]),
        pltpu.make_async_copy(lower_ref.at[pl.ds(0, W - CUT)], dst_out.at[pl.ds(CUT, W - CUT)], sem.at[1]),
    ]
    for copy in copies:
        copy.start()
    dst_state_out[...] = lower_ref[W - CUT :, :][0]
    src_out[...], _ = source_update(1, way_ref, src_ref, src_state_ref, ids_ref)
    for copy in copies:
        copy.wait()


def call(kernel, outs, *args, scalars=0, scratch=(), passes=0, spaces=None):
    shapes = [shape if isinstance(shape, jax.ShapeDtypeStruct) else jax.ShapeDtypeStruct(shape, jnp.float32) for shape in outs]
    vector = pl.BlockSpec(memory_space=pltpu.VMEM)
    scalar = pl.BlockSpec(memory_space=pltpu.SMEM)
    moved = sum(value.size * value.dtype.itemsize for value in (*args, *shapes))
    return pl.pallas_call(
        kernel,
        out_shape=shapes,
        in_specs=[scalar] * scalars + [vector] * (len(args) - scalars),
        out_specs=spaces or [vector] * len(shapes),
        scratch_shapes=scratch,
        cost_estimate=pl.CostEstimate(flops=passes * 2 * EP * EP * SLAB, bytes_accessed=moved, transcendentals=0),
        compiler_params=pltpu.CompilerParams(vmem_limit_bytes=16 * 1024 * 1024),
    )(*args)


def shifted(value, steps):
    count = lax.axis_size(RIGHT)
    pairs = [(source, (source + steps) % count) for source in range(count)]
    return lax.ppermute(value, RIGHT, pairs)


def swapped(value):
    return lax.ppermute(value, "c", [(0, 1), (1, 0)])


def exchanged(value, axes):
    return lax.all_to_all(value, axes, split_axis=0, concat_axis=0, tiled=True)


def chip_half(mine, other):
    return mine + swapped(other)


def own_part(half):
    height = W // lax.axis_size(PLANE)
    return lax.dynamic_slice_in_dim(half, lax.axis_index(PLANE) * height, height, 0).reshape(-1)


def relation_update(half, own, own_sums, upper=None, lower=None, late=None):
    lanes, layers = (lax.axis_size(PLANE), lax.axis_size(COLUMN))
    total = jnp.sum(exchanged(half.reshape(lanes, 1, -1), PLANE), axis=(0, 1))
    if upper is not None:
        total, upper = lax.optimization_barrier((total, shifted(upper, -SHIFT)))
    total = jnp.sum(exchanged(jnp.broadcast_to(total, (layers, 1, *own.shape)), COLUMN), axis=(0, 1))
    if lower is not None:
        total, lower, late = lax.optimization_barrier((total, lower, late))
        lower = shifted(lower, -SHIFT)
    own_sums = own_sums + total * total
    own = own - REL_RATE * total / jnp.sqrt(own_sums)
    half = exchanged(jnp.broadcast_to(own, (lanes, 1, *own.shape)), PLANE).reshape(W, HALF)
    return (half, own, own_sums, upper, lower, late)


def padded(value, live, low):
    picked = value[low : low + BATCH]
    spot = lax.iota(jnp.int32, BATCH) + low
    return jnp.pad(jnp.where(spot < live, picked, -1), (0, EP - BATCH), constant_values=-1)


def body(
    src_embed, src_state, dst_embed, dst_state, relation, rel_state, edge_src, edge_dst, edge_rel, neg_rows, edge_count
):
    dst_table = shifted(dst_embed.T, SHIFT)
    core = lax.axis_index("c")
    live = edge_count[0]
    near_rel = edge_rel[0] ^ (core * HALF)
    ids = jnp.stack(
        [
            padded(edge_src[0], live, 0),
            padded(edge_src[0], live, BATCH),
            padded(edge_dst[0], live, 0),
            padded(edge_dst[0], live, BATCH),
            padded(edge_rel[0], live, 0),
            padded(near_rel, live, 0),
            padded(near_rel, live, BATCH),
            jnp.full((EP,), -1, jnp.int32),
        ]
    )
    negs = jnp.pad(neg_rows[0], ((0, 0), (0, NP - NEG)), constant_values=-1)
    place = core.reshape(1).astype(jnp.int32)
    src_table, src_sums = (src_embed.T, src_state.reshape(1, SLAB))

    flat = (1, SLAB)
    sources, relations, counts, own, own_sums, dst_sums = call(
        prepare_kernel,
        [(W, EP), (W, EP), (SLAB, BATCHES), (W, HALF), (W, HALF), flat],
        place, src_table, relation.T, rel_state.T, ids, negs, dst_state.reshape(flat),
        scalars=1, passes=4,
    )
    dst_sums, own, own_sums = lax.optimization_barrier((dst_sums, own_part(own), own_part(own_sums)))
    dst_table, dst_sums = lax.optimization_barrier((dst_table, shifted(dst_sums, SHIFT)))
    kept = [
        (W, EP),
        *[jax.ShapeDtypeStruct((W, EP), jnp.bfloat16)] * 2,
        *[jax.ShapeDtypeStruct((SLAB, EP), jnp.bfloat16)] * 2,
    ]
    mine, other, *kept_values = call(
        first_relation_kernel, [(W, HALF), (W, HALF), *kept], sources, relations, dst_table, ids, counts, passes=8
    )
    half = chip_half(mine, other)
    half, *tables = lax.optimization_barrier(
        (
            half,
            *call(
                first_entity_kernel,
                [(W, SLAB), flat, (W, SLAB), flat],
                *kept_values, dst_table, dst_sums, src_table, src_sums, ids, passes=5,
            ),
        )
    )
    near, own, own_sums, *_ = relation_update(half, own, own_sums)
    near, *tables = lax.optimization_barrier((near, *tables))
    src_table, src_sums, dst_table, dst_sums = tables
    (sources,) = call(gather_kernel, [(W, EP)], src_table, ids, passes=2)
    mine, other, way, *kept_values = call(
        second_relation_kernel,
        [(W, HALF), (W, HALF), *kept],
        near, swapped(near), sources, dst_table, ids, counts, passes=10,
    )
    half = chip_half(mine, other)
    half, upper, lower = lax.optimization_barrier(
        (
            half,
            *call(
                second_target_kernel,
                [(CUT, SLAB), (W + 8 - CUT, SLAB)],
                *kept_values, dst_table, dst_sums, passes=3,
            ),
        )
    )
    near, own, own_sums, upper, lower, way = relation_update(half, own, own_sums, upper, lower, way)
    near, lower = lax.optimization_barrier((near, lower))
    vector = pl.BlockSpec(memory_space=pltpu.VMEM)
    src_table, dst_table, dst_sums = call(
        last_kernel,
        [(W, SLAB), (W, SLAB), (SLAB,)],
        way, src_table, src_sums, ids, upper, lower,
        scratch=[pltpu.SemaphoreType.DMA((2,))], passes=2, spaces=[vector, pl.BlockSpec(memory_space=pl.ANY), vector],
    )
    far = swapped(near)
    first = core == 0
    relation = jnp.concatenate([jnp.where(first, near, far), jnp.where(first, far, near)], axis=1)
    return (src_table.T, dst_table.T, dst_sums, relation.T)


def solution(mesh):
    left, right = (mesh.shape["left"], mesh.shape["right"])
    devices = mesh.devices.reshape(left // 2, 2, 4, right // 8, 2)
    inner = Mesh(devices, AXES)
    in_specs = (
        P(AXES, None),
        P(AXES),
        P(AXES, None),
        P(AXES),
        P(),
        P(),
        P(AXES, None),
        P(AXES, None),
        P(AXES, None),
        P(AXES, None, None),
        P(AXES),
    )
    out_specs = (P(AXES, None), P(AXES, None), P(AXES), P())
    return jax.shard_map(body, mesh=inner, in_specs=in_specs, out_specs=out_specs, check_vma=False)
```

```python
import jax
import jax.numpy as jnp
from jax import lax
from jax.experimental import pallas as pl
from jax.experimental.pallas import tpu as pltpu
from jax.sharding import Mesh, PartitionSpec as P

BATCH = 500
BATCHES = 2
NEG = 1000
SHIFT = 5
SLAB = 384
REL = 256
HALF = 128
W = 400
MID = 200
EP = 512
NP = 1024
CUT = 200

ROW_RATE = 0.2
REL_RATE = 1.0

AXES = ("x", "zh", "y", "zl", "c")
PLANE = ("y", "x")
COLUMN = ("zl", "zh")
RIGHT = ("y", "zl", "c")

NN = (((1,), (0,)), ((), ()))
NT = (((1,), (1,)), ((), ()))
TN = (((0,), (0,)), ((), ()))


def parts(value):
    high = value.astype(jnp.bfloat16)
    low = (value - high.astype(jnp.float32)).astype(jnp.bfloat16)
    return (high, low)


def dot(first, second, dims):
    return lax.dot_general(first, second, dims, preferred_element_type=jnp.float32)


def joined(values, axis):
    return jnp.concatenate(values, axis=axis)


def dot3(first, second, dims):
    (one,), (two,) = dims[0]
    return dot(joined([first[0], first[0], first[1]], one), joined([second[0], second[1], second[0]], two), dims)


def pick(rows, ids):
    return (lax.broadcasted_iota(jnp.int32, (rows, EP), 0) == ids).astype(jnp.bfloat16)


def gather(table, hot):
    return dot(joined(parts(table), 1), joined([hot, hot], 0), NN)


def scatter(values, hot):
    high, low = parts(values)
    return dot(high, hot, NT) + dot(low, hot, NT)


def entity_update(table, state, grad):
    state = state + jnp.sum(grad * grad, axis=0, keepdims=True) * (1.0 / W)
    return (table - grad * (ROW_RATE / jnp.sqrt(state)), state)


def query(sources, relations):
    s_re, s_im = (sources[:MID], sources[MID:])
    r_re, r_im = (relations[:MID], relations[MID:])
    return parts(jnp.concatenate([s_re * r_re - s_im * r_im, s_re * r_im + s_im * r_re], axis=0))


def against(grads, other):
    g_re, g_im = (grads[:MID], grads[MID:])
    o_re, o_im = (other[:MID], other[MID:])
    return jnp.concatenate([g_re * o_re + g_im * o_im, g_im * o_re - g_re * o_im], axis=0)


def edge_weights(logits, dst_ids, counts):
    hit = lax.broadcasted_iota(jnp.int32, (SLAB, EP), 0) == dst_ids
    positive = jnp.where(hit, 0.5, 0.0)
    return parts((counts - positive) + (counts + positive) * jnp.tanh(0.5 * logits))


def put(refs, values):
    for ref, value in zip(refs, values, strict=True):
        ref[...] = value


def put(refs, values):
    for ref, value in zip(refs, values, strict=True):
        ref[...] = value


def relation_side(
    batch, queries, sources, relations, dst_ref, ids_ref, counts_ref, mine_ref, other_ref, way_ref, weight_refs
):
    rows = parts(dst_ref[...])
    dst_ids = ids_ref[2 + batch : 3 + batch, :]
    weights = edge_weights(dot3(rows, queries, TN), dst_ids, counts_ref[:, batch : batch + 1])
    put(weight_refs, weights)
    grads = dot3(rows, weights, NN)
    rel_grad = scatter(against(grads, sources), pick(REL, ids_ref[5 + batch : 6 + batch, :]))
    put((mine_ref, other_ref), (rel_grad[:, :HALF], rel_grad[:, HALF:]))
    way_ref[...] = against(grads, relations)


def target_update(query_refs, weight_refs, dst_ref, dst_state_ref):
    queries, weights = [tuple(ref[...] for ref in refs) for refs in (query_refs, weight_refs)]
    return entity_update(dst_ref[...], dst_state_ref[...], dot3(queries, weights, NT))


def source_update(batch, way_ref, src_ref, src_state_ref, ids_ref):
    src_grad = scatter(way_ref[...], pick(SLAB, ids_ref[batch : batch + 1, :]))
    return entity_update(src_ref[...], src_state_ref[...], src_grad)


def prepare_kernel(
    place_ref, src_ref, rel_ref, rel_state_ref, ids_ref, neg_ref, dst_state_ref,
    sources_ref, relations_ref, high_ref, low_ref, counts_ref, own_ref, own_sums_ref, dst_state_out,
):
    sources = gather(src_ref[...], pick(SLAB, ids_ref[0:1, :]))
    relations = gather(rel_ref[...], pick(REL, ids_ref[4:5, :]))
    put((sources_ref, relations_ref), (sources, relations))
    put((high_ref, low_ref), query(sources, relations))
    for batch in range(BATCHES):
        same = lax.broadcasted_iota(jnp.int32, (SLAB, NP), 0) == neg_ref[batch : batch + 1, :]
        total = jnp.sum(jnp.where(same, 1.0, 0.0), axis=1, keepdims=True)
        counts_ref[:, batch : batch + 1] = total * (0.5 / NEG)
    for source, target in ((rel_ref, own_ref), (rel_state_ref, own_sums_ref)):
        target[...] = jnp.where(place_ref[0] == 0, source[:, :HALF], source[:, HALF:])
    dst_state_out[...] = dst_state_ref[...]


def first_relation_kernel(
    high_ref, low_ref, sources_ref, relations_ref, dst_ref, ids_ref, counts_ref, mine_ref, other_ref, way_ref, *weight_refs
):
    relation_side(
        0, (high_ref[...], low_ref[...]), sources_ref[...], relations_ref[...], dst_ref, ids_ref, counts_ref,
        mine_ref, other_ref, way_ref, weight_refs,
    )


def first_entity_kernel(
    way_ref, high_ref, low_ref, weight_high_ref, weight_low_ref, dst_ref, dst_state_ref, src_ref, src_state_ref, ids_ref,
    src_out, src_state_out, dst_out, dst_state_out,
):
    src_out[...], src_state_out[...] = source_update(0, way_ref, src_ref, src_state_ref, ids_ref)
    dst_out[...], dst_state_out[...] = target_update(
        (high_ref, low_ref), (weight_high_ref, weight_low_ref), dst_ref, dst_state_ref
    )


def gather_kernel(src_ref, ids_ref, sources_ref):
    sources_ref[...] = gather(src_ref[...], pick(SLAB, ids_ref[1:2, :]))


def second_relation_kernel(
    rel_mine_ref, rel_other_ref, sources_ref, dst_ref, ids_ref, counts_ref,
    mine_ref, other_ref, way_ref, weight_high_ref, weight_low_ref, high_ref, low_ref,
):
    relation = jnp.concatenate([rel_mine_ref[...], rel_other_ref[...]], axis=1)
    sources, relations = (sources_ref[...], gather(relation, pick(REL, ids_ref[6:7, :])))
    queries = query(sources, relations)
    put((high_ref, low_ref), queries)
    relation_side(
        1, queries, sources, relations, dst_ref, ids_ref, counts_ref,
        mine_ref, other_ref, way_ref, (weight_high_ref, weight_low_ref),
    )


def second_target_kernel(
    high_ref, low_ref, weight_high_ref, weight_low_ref, dst_ref, dst_state_ref, upper_out, lower_out
):
    dst_table, dst_state = target_update((high_ref, low_ref), (weight_high_ref, weight_low_ref), dst_ref, dst_state_ref)
    upper_out[...] = dst_table[:CUT]
    lower_out[: W - CUT, :] = dst_table[CUT:]
    lower_out[W - CUT :, :] = jnp.broadcast_to(dst_state, (8, SLAB))


def last_kernel(
    way_ref, src_ref, src_state_ref, ids_ref, upper_ref, lower_ref, src_out, dst_out, dst_state_out, sem
):
    copies = [
        pltpu.make_async_copy(upper_ref, dst_out.at[pl.ds(0, CUT)], sem.at[0]),
        pltpu.make_async_copy(lower_ref.at[pl.ds(0, W - CUT)], dst_out.at[pl.ds(CUT, W - CUT)], sem.at[1]),
    ]
    for copy in copies:
        copy.start()
    dst_state_out[...] = lower_ref[W - CUT :, :][0]
    src_out[...], _ = source_update(1, way_ref, src_ref, src_state_ref, ids_ref)
    for copy in copies:
        copy.wait()


def call(kernel, outs, *args, scalars=0, scratch=(), passes=0, spaces=None):
    shapes = [shape if isinstance(shape, jax.ShapeDtypeStruct) else jax.ShapeDtypeStruct(shape, jnp.float32) for shape in outs]
    vector = pl.BlockSpec(memory_space=pltpu.VMEM)
    scalar = pl.BlockSpec(memory_space=pltpu.SMEM)
    moved = sum(value.size * value.dtype.itemsize for value in (*args, *shapes))
    return pl.pallas_call(
        kernel,
        out_shape=shapes,
        in_specs=[scalar] * scalars + [vector] * (len(args) - scalars),
        out_specs=spaces or [vector] * len(shapes),
        scratch_shapes=scratch,
        cost_estimate=pl.CostEstimate(flops=passes * 2 * EP * EP * SLAB, bytes_accessed=moved, transcendentals=0),
        compiler_params=pltpu.CompilerParams(vmem_limit_bytes=16 * 1024 * 1024),
    )(*args)


def shifted(value, steps):
    count = lax.axis_size(RIGHT)
    pairs = [(source, (source + steps) % count) for source in range(count)]
    return lax.ppermute(value, RIGHT, pairs)


def swapped(value):
    return lax.ppermute(value, "c", [(0, 1), (1, 0)])


def exchanged(value, axes):
    return lax.all_to_all(value, axes, split_axis=0, concat_axis=0, tiled=True)


def chip_half(mine, other):
    return mine + swapped(other)


def own_part(half):
    height = W // lax.axis_size(PLANE)
    return lax.dynamic_slice_in_dim(half, lax.axis_index(PLANE) * height, height, 0).reshape(-1)


def relation_update(half, own, own_sums, upper=None, lower=None, late=None):
    lanes, layers = (lax.axis_size(PLANE), lax.axis_size(COLUMN))
    total = jnp.sum(exchanged(half.reshape(lanes, 1, -1), PLANE), axis=(0, 1))
    if upper is not None:
        total, upper = lax.optimization_barrier((total, shifted(upper, -SHIFT)))
    total = jnp.sum(exchanged(jnp.broadcast_to(total, (layers, 1, *own.shape)), COLUMN), axis=(0, 1))
    if lower is not None:
        total, lower, late = lax.optimization_barrier((total, lower, late))
        lower = shifted(lower, -SHIFT)
    own_sums = own_sums + total * total
    own = own - REL_RATE * total / jnp.sqrt(own_sums)
    half = exchanged(jnp.broadcast_to(own, (lanes, 1, *own.shape)), PLANE).reshape(W, HALF)
    return (half, own, own_sums, upper, lower, late)


def padded(value, live, low):
    picked = value[low : low + BATCH]
    spot = lax.iota(jnp.int32, BATCH) + low
    return jnp.pad(jnp.where(spot < live, picked, -1), (0, EP - BATCH), constant_values=-1)


def body(
    src_embed, src_state, dst_embed, dst_state, relation, rel_state, edge_src, edge_dst, edge_rel, neg_rows, edge_count
):
    dst_table = shifted(dst_embed.T, SHIFT)
    core = lax.axis_index("c")
    live = edge_count[0]
    near_rel = edge_rel[0] ^ (core * HALF)
    ids = jnp.stack(
        [
            padded(edge_src[0], live, 0),
            padded(edge_src[0], live, BATCH),
            padded(edge_dst[0], live, 0),
            padded(edge_dst[0], live, BATCH),
            padded(edge_rel[0], live, 0),
            padded(near_rel, live, 0),
            padded(near_rel, live, BATCH),
            jnp.full((EP,), -1, jnp.int32),
        ]
    )
    negs = jnp.pad(neg_rows[0], ((0, 0), (0, NP - NEG)), constant_values=-1)
    place = core.reshape(1).astype(jnp.int32)
    src_table, src_sums = (src_embed.T, src_state.reshape(1, SLAB))

    flat = (1, SLAB)
    query_shapes = [jax.ShapeDtypeStruct((W, EP), jnp.bfloat16)] * 2
    weight_shapes = [jax.ShapeDtypeStruct((SLAB, EP), jnp.bfloat16)] * 2
    sources, relations, high, low, counts, own, own_sums, dst_sums = call(
        prepare_kernel,
        [(W, EP), (W, EP), *query_shapes, (SLAB, BATCHES), (W, HALF), (W, HALF), flat],
        place, src_table, relation.T, rel_state.T, ids, negs, dst_state.reshape(flat),
        scalars=1, passes=4,
    )
    dst_sums, own, own_sums = lax.optimization_barrier((dst_sums, own_part(own), own_part(own_sums)))
    dst_table, dst_sums = lax.optimization_barrier((dst_table, shifted(dst_sums, SHIFT)))
    mine, other, way, *weights = call(
        first_relation_kernel,
        [(W, HALF), (W, HALF), (W, EP), *weight_shapes],
        high, low, sources, relations, dst_table, ids, counts, passes=8,
    )
    half = chip_half(mine, other)
    half, *tables = lax.optimization_barrier(
        (
            half,
            *call(
                first_entity_kernel,
                [(W, SLAB), flat, (W, SLAB), flat],
                way, high, low, *weights, dst_table, dst_sums, src_table, src_sums, ids, passes=5,
            ),
        )
    )
    near, own, own_sums, *_ = relation_update(half, own, own_sums)
    near, src_table, src_sums, dst_table, dst_sums = lax.optimization_barrier((near, *tables))
    (sources,) = call(gather_kernel, [(W, EP)], src_table, ids, passes=2)
    mine, other, way, weight_high, weight_low, high, low = call(
        second_relation_kernel,
        [(W, HALF), (W, HALF), (W, EP), *weight_shapes, *query_shapes],
        near, swapped(near), sources, dst_table, ids, counts, passes=10,
    )
    half = chip_half(mine, other)
    half, upper, lower = lax.optimization_barrier(
        (
            half,
            *call(
                second_target_kernel,
                [(CUT, SLAB), (W + 8 - CUT, SLAB)],
                high, low, weight_high, weight_low, dst_table, dst_sums, passes=3,
            ),
        )
    )
    near, own, own_sums, upper, lower, way = relation_update(half, own, own_sums, upper, lower, way)
    near, lower = lax.optimization_barrier((near, lower))
    vector = pl.BlockSpec(memory_space=pltpu.VMEM)
    src_table, dst_table, dst_sums = call(
        last_kernel,
        [(W, SLAB), (W, SLAB), (SLAB,)],
        way, src_table, src_sums, ids, upper, lower,
        scratch=[pltpu.SemaphoreType.DMA((2,))], passes=2, spaces=[vector, pl.BlockSpec(memory_space=pl.ANY), vector],
    )
    far = swapped(near)
    first = core == 0
    relation = jnp.concatenate([jnp.where(first, near, far), jnp.where(first, far, near)], axis=1)
    return (src_table.T, dst_table.T, dst_sums, relation.T)


def solution(mesh):
    left, right = (mesh.shape["left"], mesh.shape["right"])
    devices = mesh.devices.reshape(left // 2, 2, 4, right // 8, 2)
    inner = Mesh(devices, AXES)
    in_specs = (
        P(AXES, None),
        P(AXES),
        P(AXES, None),
        P(AXES),
        P(),
        P(),
        P(AXES, None),
        P(AXES, None),
        P(AXES, None),
        P(AXES, None, None),
        P(AXES),
    )
    out_specs = (P(AXES, None), P(AXES, None), P(AXES), P())
    return jax.shard_map(body, mesh=inner, in_specs=in_specs, out_specs=out_specs, check_vma=False)
```

```python
import jax
import jax.numpy as jnp
from jax import lax
from jax.experimental import pallas as pl
from jax.experimental.pallas import tpu as pltpu
from jax.sharding import Mesh, PartitionSpec as P

BATCH = 500
BATCHES = 2
NEG = 1000
SHIFT = 5
SLAB = 384
REL = 256
HALF = 128
W = 400
MID = 200
EP = 512
NP = 1024
CUT = 200

ROW_RATE = 0.2
REL_RATE = 1.0

AXES = ("x", "zh", "y", "zl", "c")
PLANE = ("y", "x")
COLUMN = ("zl", "zh")
RIGHT = ("y", "zl", "c")

NN = (((1,), (0,)), ((), ()))
NT = (((1,), (1,)), ((), ()))
TN = (((0,), (0,)), ((), ()))


def parts(value):
    high = value.astype(jnp.bfloat16)
    low = (value - high.astype(jnp.float32)).astype(jnp.bfloat16)
    return (high, low)


def dot(first, second, dims):
    return lax.dot_general(first, second, dims, preferred_element_type=jnp.float32)


def joined(values, axis):
    return jnp.concatenate(values, axis=axis)


def dot3(first, second, dims):
    (one,), (two,) = dims[0]
    return dot(joined([first[0], first[0], first[1]], one), joined([second[0], second[1], second[0]], two), dims)


def pick(rows, ids):
    return (lax.broadcasted_iota(jnp.int32, (rows, EP), 0) == ids).astype(jnp.bfloat16)


def gather(table, hot):
    return dot(joined(parts(table), 1), joined([hot, hot], 0), NN)


def scatter(values, hot):
    high, low = parts(values)
    return dot(high, hot, NT) + dot(low, hot, NT)


def entity_update(table, state, grad):
    state = state + jnp.sum(grad * grad, axis=0, keepdims=True) * (1.0 / W)
    return (table - grad * (ROW_RATE / jnp.sqrt(state)), state)


def query(sources, relations):
    s_re, s_im = (sources[:MID], sources[MID:])
    r_re, r_im = (relations[:MID], relations[MID:])
    return parts(jnp.concatenate([s_re * r_re - s_im * r_im, s_re * r_im + s_im * r_re], axis=0))


def against(grads, other):
    g_re, g_im = (grads[:MID], grads[MID:])
    o_re, o_im = (other[:MID], other[MID:])
    return jnp.concatenate([g_re * o_re + g_im * o_im, g_im * o_re - g_re * o_im], axis=0)


def edge_weights(logits, dst_ids, counts):
    hit = lax.broadcasted_iota(jnp.int32, (SLAB, EP), 0) == dst_ids
    positive = jnp.where(hit, 0.5, 0.0)
    return parts((counts - positive) + (counts + positive) * jnp.tanh(0.5 * logits))


def put(refs, values):
    for ref, value in zip(refs, values, strict=True):
        ref[...] = value


def put(refs, values):
    for ref, value in zip(refs, values, strict=True):
        ref[...] = value


def relation_side(
    batch, queries, sources, relations, dst_ref, ids_ref, counts_ref, mine_ref, other_ref, way_ref
):
    rows = parts(dst_ref[...])
    dst_ids = ids_ref[2 + batch : 3 + batch, :]
    weights = edge_weights(dot3(rows, queries, TN), dst_ids, counts_ref[:, batch : batch + 1])
    grads = dot3(rows, weights, NN)
    rel_grad = scatter(against(grads, sources), pick(REL, ids_ref[5 + batch : 6 + batch, :]))
    put((mine_ref, other_ref), (rel_grad[:, :HALF], rel_grad[:, HALF:]))
    way_ref[...] = against(grads, relations)
    return weights


def target_update(queries, weights, dst_ref, dst_state_ref):
    return entity_update(dst_ref[...], dst_state_ref[...], dot3(queries, weights, NT))


def source_update(batch, way_ref, src_ref, src_state_ref, ids_ref):
    src_grad = scatter(way_ref[...], pick(SLAB, ids_ref[batch : batch + 1, :]))
    return entity_update(src_ref[...], src_state_ref[...], src_grad)


def prepare_kernel(
    place_ref, src_ref, rel_ref, rel_state_ref, ids_ref, neg_ref, dst_state_ref,
    sources_ref, relations_ref, high_ref, low_ref, counts_ref, own_ref, own_sums_ref, dst_state_out,
):
    sources = gather(src_ref[...], pick(SLAB, ids_ref[0:1, :]))
    relations = gather(rel_ref[...], pick(REL, ids_ref[4:5, :]))
    put((sources_ref, relations_ref), (sources, relations))
    put((high_ref, low_ref), query(sources, relations))
    for batch in range(BATCHES):
        same = lax.broadcasted_iota(jnp.int32, (SLAB, NP), 0) == neg_ref[batch : batch + 1, :]
        total = jnp.sum(jnp.where(same, 1.0, 0.0), axis=1, keepdims=True)
        counts_ref[:, batch : batch + 1] = total * (0.5 / NEG)
    for source, target in ((rel_ref, own_ref), (rel_state_ref, own_sums_ref)):
        target[...] = jnp.where(place_ref[0] == 0, source[:, :HALF], source[:, HALF:])
    dst_state_out[...] = dst_state_ref[...]


def first_relation_kernel(
    high_ref, low_ref, sources_ref, relations_ref, dst_ref, ids_ref, counts_ref, mine_ref, other_ref, way_ref, *weight_refs
):
    weights = relation_side(
        0, (high_ref[...], low_ref[...]), sources_ref[...], relations_ref[...], dst_ref, ids_ref, counts_ref,
        mine_ref, other_ref, way_ref,
    )
    put(weight_refs, weights)


def first_entity_kernel(
    way_ref, high_ref, low_ref, weight_high_ref, weight_low_ref, dst_ref, dst_state_ref, src_ref, src_state_ref, ids_ref,
    src_out, src_state_out, dst_out, dst_state_out,
):
    src_out[...], src_state_out[...] = source_update(0, way_ref, src_ref, src_state_ref, ids_ref)
    queries, weights = ((high_ref[...], low_ref[...]), (weight_high_ref[...], weight_low_ref[...]))
    dst_out[...], dst_state_out[...] = target_update(queries, weights, dst_ref, dst_state_ref)


def gather_kernel(src_ref, ids_ref, sources_ref):
    sources_ref[...] = gather(src_ref[...], pick(SLAB, ids_ref[1:2, :]))


def second_kernel(
    rel_mine_ref, rel_other_ref, sources_ref, dst_ref, dst_state_ref, ids_ref, counts_ref,
    mine_ref, other_ref, way_ref, upper_out, lower_out,
):
    relation = jnp.concatenate([rel_mine_ref[...], rel_other_ref[...]], axis=1)
    sources, relations = (sources_ref[...], gather(relation, pick(REL, ids_ref[6:7, :])))
    queries = query(sources, relations)
    weights = relation_side(
        1, queries, sources, relations, dst_ref, ids_ref, counts_ref, mine_ref, other_ref, way_ref
    )
    dst_table, dst_state = target_update(queries, weights, dst_ref, dst_state_ref)
    upper_out[...] = dst_table[:CUT]
    lower_out[: W - CUT, :] = dst_table[CUT:]
    lower_out[W - CUT :, :] = jnp.broadcast_to(dst_state, (8, SLAB))


def last_kernel(
    way_ref, src_ref, src_state_ref, ids_ref, upper_ref, lower_ref, src_out, dst_out, dst_state_out, sem
):
    copies = [
        pltpu.make_async_copy(upper_ref, dst_out.at[pl.ds(0, CUT)], sem.at[0]),
        pltpu.make_async_copy(lower_ref.at[pl.ds(0, W - CUT)], dst_out.at[pl.ds(CUT, W - CUT)], sem.at[1]),
    ]
    for copy in copies:
        copy.start()
    dst_state_out[...] = lower_ref[W - CUT :, :][0]
    src_out[...], _ = source_update(1, way_ref, src_ref, src_state_ref, ids_ref)
    for copy in copies:
        copy.wait()


def call(kernel, outs, *args, scalars=0, scratch=(), passes=0, spaces=None):
    shapes = [shape if isinstance(shape, jax.ShapeDtypeStruct) else jax.ShapeDtypeStruct(shape, jnp.float32) for shape in outs]
    vector = pl.BlockSpec(memory_space=pltpu.VMEM)
    scalar = pl.BlockSpec(memory_space=pltpu.SMEM)
    moved = sum(value.size * value.dtype.itemsize for value in (*args, *shapes))
    return pl.pallas_call(
        kernel,
        out_shape=shapes,
        in_specs=[scalar] * scalars + [vector] * (len(args) - scalars),
        out_specs=spaces or [vector] * len(shapes),
        scratch_shapes=scratch,
        cost_estimate=pl.CostEstimate(flops=passes * 2 * EP * EP * SLAB, bytes_accessed=moved, transcendentals=0),
        compiler_params=pltpu.CompilerParams(vmem_limit_bytes=16 * 1024 * 1024),
    )(*args)


def shifted(value, steps):
    count = lax.axis_size(RIGHT)
    pairs = [(source, (source + steps) % count) for source in range(count)]
    return lax.ppermute(value, RIGHT, pairs)


def swapped(value):
    return lax.ppermute(value, "c", [(0, 1), (1, 0)])


def exchanged(value, axes):
    return lax.all_to_all(value, axes, split_axis=0, concat_axis=0, tiled=True)


def chip_half(mine, other):
    return mine + swapped(other)


def own_part(half):
    height = W // lax.axis_size(PLANE)
    return lax.dynamic_slice_in_dim(half, lax.axis_index(PLANE) * height, height, 0).reshape(-1)


def relation_update(half, own, own_sums, upper=None, lower=None, late=None):
    lanes, layers = (lax.axis_size(PLANE), lax.axis_size(COLUMN))
    total = jnp.sum(exchanged(half.reshape(lanes, 1, -1), PLANE), axis=(0, 1))
    if upper is not None:
        total, upper = lax.optimization_barrier((total, shifted(upper, -SHIFT)))
    total = jnp.sum(exchanged(jnp.broadcast_to(total, (layers, 1, *own.shape)), COLUMN), axis=(0, 1))
    if lower is not None:
        total, lower, late = lax.optimization_barrier((total, lower, late))
        lower = shifted(lower, -SHIFT)
    own_sums = own_sums + total * total
    own = own - REL_RATE * total / jnp.sqrt(own_sums)
    half = exchanged(jnp.broadcast_to(own, (lanes, 1, *own.shape)), PLANE).reshape(W, HALF)
    return (half, own, own_sums, upper, lower, late)


def padded(value, live, low):
    picked = value[low : low + BATCH]
    spot = lax.iota(jnp.int32, BATCH) + low
    return jnp.pad(jnp.where(spot < live, picked, -1), (0, EP - BATCH), constant_values=-1)


def body(
    src_embed, src_state, dst_embed, dst_state, relation, rel_state, edge_src, edge_dst, edge_rel, neg_rows, edge_count
):
    dst_table = shifted(dst_embed.T, SHIFT)
    core = lax.axis_index("c")
    live = edge_count[0]
    near_rel = edge_rel[0] ^ (core * HALF)
    ids = jnp.stack(
        [
            padded(edge_src[0], live, 0),
            padded(edge_src[0], live, BATCH),
            padded(edge_dst[0], live, 0),
            padded(edge_dst[0], live, BATCH),
            padded(edge_rel[0], live, 0),
            padded(near_rel, live, 0),
            padded(near_rel, live, BATCH),
            jnp.full((EP,), -1, jnp.int32),
        ]
    )
    negs = jnp.pad(neg_rows[0], ((0, 0), (0, NP - NEG)), constant_values=-1)
    place = core.reshape(1).astype(jnp.int32)
    src_table, src_sums = (src_embed.T, src_state.reshape(1, SLAB))

    flat = (1, SLAB)
    query_shapes = [jax.ShapeDtypeStruct((W, EP), jnp.bfloat16)] * 2
    weight_shapes = [jax.ShapeDtypeStruct((SLAB, EP), jnp.bfloat16)] * 2
    sources, relations, high, low, counts, own, own_sums, dst_sums = call(
        prepare_kernel,
        [(W, EP), (W, EP), *query_shapes, (SLAB, BATCHES), (W, HALF), (W, HALF), flat],
        place, src_table, relation.T, rel_state.T, ids, negs, dst_state.reshape(flat),
        scalars=1, passes=4,
    )
    dst_sums, own, own_sums = lax.optimization_barrier((dst_sums, own_part(own), own_part(own_sums)))
    dst_table, dst_sums = lax.optimization_barrier((dst_table, shifted(dst_sums, SHIFT)))
    mine, other, way, *weights = call(
        first_relation_kernel,
        [(W, HALF), (W, HALF), (W, EP), *weight_shapes],
        high, low, sources, relations, dst_table, ids, counts, passes=8,
    )
    half = chip_half(mine, other)
    half, *tables = lax.optimization_barrier(
        (
            half,
            *call(
                first_entity_kernel,
                [(W, SLAB), flat, (W, SLAB), flat],
                way, high, low, *weights, dst_table, dst_sums, src_table, src_sums, ids, passes=5,
            ),
        )
    )
    near, own, own_sums, *_ = relation_update(half, own, own_sums)
    near, src_table, src_sums, dst_table, dst_sums = lax.optimization_barrier((near, *tables))
    (sources,) = call(gather_kernel, [(W, EP)], src_table, ids, passes=2)
    mine, other, way, upper, lower = call(
        second_kernel,
        [(W, HALF), (W, HALF), (W, EP), (CUT, SLAB), (W + 8 - CUT, SLAB)],
        near, swapped(near), sources, dst_table, dst_sums, ids, counts, passes=13,
    )
    half = chip_half(mine, other)
    near, own, own_sums, upper, lower, way = relation_update(half, own, own_sums, upper, lower, way)
    near, lower = lax.optimization_barrier((near, lower))
    vector = pl.BlockSpec(memory_space=pltpu.VMEM)
    src_table, dst_table, dst_sums = call(
        last_kernel,
        [(W, SLAB), (W, SLAB), (SLAB,)],
        way, src_table, src_sums, ids, upper, lower,
        scratch=[pltpu.SemaphoreType.DMA((2,))], passes=2, spaces=[vector, pl.BlockSpec(memory_space=pl.ANY), vector],
    )
    far = swapped(near)
    first = core == 0
    relation = jnp.concatenate([jnp.where(first, near, far), jnp.where(first, far, near)], axis=1)
    return (src_table.T, dst_table.T, dst_sums, relation.T)


def solution(mesh):
    left, right = (mesh.shape["left"], mesh.shape["right"])
    devices = mesh.devices.reshape(left // 2, 2, 4, right // 8, 2)
    inner = Mesh(devices, AXES)
    in_specs = (
        P(AXES, None),
        P(AXES),
        P(AXES, None),
        P(AXES),
        P(),
        P(),
        P(AXES, None),
        P(AXES, None),
        P(AXES, None),
        P(AXES, None, None),
        P(AXES),
    )
    out_specs = (P(AXES, None), P(AXES, None), P(AXES), P())
    return jax.shard_map(body, mesh=inner, in_specs=in_specs, out_specs=out_specs, check_vma=False)
```

```python
import jax
import jax.numpy as jnp
from jax import lax
from jax.experimental import pallas as pl
from jax.experimental.pallas import tpu as pltpu
from jax.sharding import Mesh, PartitionSpec as P

BATCH = 500
BATCHES = 2
NEG = 1000
SHIFT = 5
SLAB = 384
REL = 256
HALF = 128
W = 400
MID = 200
EP = 512
NP = 1024
CUT = 200

ROW_RATE = 0.2
REL_RATE = 1.0

AXES = ("x", "zh", "y", "zl", "c")
PLANE = ("y", "x")
COLUMN = ("zl", "zh")
RIGHT = ("y", "zl", "c")

NN = (((1,), (0,)), ((), ()))
NT = (((1,), (1,)), ((), ()))
TN = (((0,), (0,)), ((), ()))


def parts(value):
    high = value.astype(jnp.bfloat16)
    low = (value - high.astype(jnp.float32)).astype(jnp.bfloat16)
    return (high, low)


def dot(first, second, dims):
    return lax.dot_general(first, second, dims, preferred_element_type=jnp.float32)


def joined(values, axis):
    return jnp.concatenate(values, axis=axis)


def dot3(first, second, dims):
    (one,), (two,) = dims[0]
    return dot(joined([first[0], first[0], first[1]], one), joined([second[0], second[1], second[0]], two), dims)


def pick(rows, ids):
    return (lax.broadcasted_iota(jnp.int32, (rows, EP), 0) == ids).astype(jnp.bfloat16)


def gather(table, hot):
    return dot(joined(parts(table), 1), joined([hot, hot], 0), NN)


def scatter(values, hot):
    high, low = parts(values)
    return dot(high, hot, NT) + dot(low, hot, NT)


def entity_update(table, state, grad):
    state = state + jnp.sum(grad * grad, axis=0, keepdims=True) * (1.0 / W)
    return (table - grad * (ROW_RATE / jnp.sqrt(state)), state)


def query(sources, relations):
    s_re, s_im = (sources[:MID], sources[MID:])
    r_re, r_im = (relations[:MID], relations[MID:])
    return parts(jnp.concatenate([s_re * r_re - s_im * r_im, s_re * r_im + s_im * r_re], axis=0))


def against(grads, other):
    g_re, g_im = (grads[:MID], grads[MID:])
    o_re, o_im = (other[:MID], other[MID:])
    return jnp.concatenate([g_re * o_re + g_im * o_im, g_im * o_re - g_re * o_im], axis=0)


def edge_weights(logits, dst_ids, counts):
    hit = lax.broadcasted_iota(jnp.int32, (SLAB, EP), 0) == dst_ids
    positive = jnp.where(hit, 0.5, 0.0)
    return parts((counts - positive) + (counts + positive) * jnp.tanh(0.5 * logits))


def put(refs, values):
    for ref, value in zip(refs, values, strict=True):
        ref[...] = value


def put(refs, values):
    for ref, value in zip(refs, values, strict=True):
        ref[...] = value


def relation_side(
    batch, queries, sources, relations, rows, logits, ids_ref, counts_ref, mine_ref, other_ref, way_ref
):
    dst_ids = ids_ref[2 + batch : 3 + batch, :]
    weights = edge_weights(logits, dst_ids, counts_ref[:, batch : batch + 1])
    grads = dot3(rows, weights, NN)
    rel_grad = scatter(against(grads, sources), pick(REL, ids_ref[5 + batch : 6 + batch, :]))
    put((mine_ref, other_ref), (rel_grad[:, :HALF], rel_grad[:, HALF:]))
    way_ref[...] = against(grads, relations)
    return weights


def target_update(queries, weights, dst_ref, dst_state_ref):
    return entity_update(dst_ref[...], dst_state_ref[...], dot3(queries, weights, NT))


def source_update(batch, way_ref, src_ref, src_state_ref, ids_ref):
    src_grad = scatter(way_ref[...], pick(SLAB, ids_ref[batch : batch + 1, :]))
    return entity_update(src_ref[...], src_state_ref[...], src_grad)


def prepare_kernel(
    place_ref, src_ref, rel_ref, rel_state_ref, ids_ref, neg_ref, dst_state_ref,
    sources_ref, relations_ref, high_ref, low_ref, counts_ref, own_ref, own_sums_ref, dst_state_out,
):
    sources = gather(src_ref[...], pick(SLAB, ids_ref[0:1, :]))
    relations = gather(rel_ref[...], pick(REL, ids_ref[4:5, :]))
    put((sources_ref, relations_ref), (sources, relations))
    put((high_ref, low_ref), query(sources, relations))
    for batch in range(BATCHES):
        same = lax.broadcasted_iota(jnp.int32, (SLAB, NP), 0) == neg_ref[batch : batch + 1, :]
        total = jnp.sum(jnp.where(same, 1.0, 0.0), axis=1, keepdims=True)
        counts_ref[:, batch : batch + 1] = total * (0.5 / NEG)
    for source, target in ((rel_ref, own_ref), (rel_state_ref, own_sums_ref)):
        target[...] = jnp.where(place_ref[0] == 0, source[:, :HALF], source[:, HALF:])
    dst_state_out[...] = dst_state_ref[...]


def first_relation_kernel(
    high_ref, low_ref, sources_ref, relations_ref, dst_ref, ids_ref, counts_ref, mine_ref, other_ref, way_ref, *weight_refs
):
    queries, rows = ((high_ref[...], low_ref[...]), parts(dst_ref[...]))
    weights = relation_side(
        0, queries, sources_ref[...], relations_ref[...], rows, dot3(rows, queries, TN), ids_ref, counts_ref,
        mine_ref, other_ref, way_ref,
    )
    put(weight_refs, weights)


def first_entity_kernel(
    way_ref, high_ref, low_ref, weight_high_ref, weight_low_ref, dst_ref, dst_state_ref, src_ref, src_state_ref, ids_ref,
    src_out, src_state_out, dst_out, dst_state_out,
):
    src_out[...], src_state_out[...] = source_update(0, way_ref, src_ref, src_state_ref, ids_ref)
    queries, weights = ((high_ref[...], low_ref[...]), (weight_high_ref[...], weight_low_ref[...]))
    dst_out[...], dst_state_out[...] = target_update(queries, weights, dst_ref, dst_state_ref)


def gather_kernel(src_ref, near_ref, dst_ref, ids_ref, sources_ref, near_rows_ref, *row_refs):
    sources_ref[...] = gather(src_ref[...], pick(SLAB, ids_ref[1:2, :]))
    near_rows_ref[...] = gather(near_ref[...], pick(HALF, ids_ref[6:7, :]))
    rows = parts(dst_ref[...])
    put(row_refs, (*rows, *[jnp.transpose(part) for part in rows]))


def second_kernel(
    far_ref, near_rows_ref, sources_ref, high_ref, low_ref, high_across_ref, low_across_ref, dst_ref, dst_state_ref,
    ids_ref, counts_ref, mine_ref, other_ref, way_ref, upper_out, lower_out,
):
    sources = sources_ref[...]
    relations = near_rows_ref[...] + gather(far_ref[...], pick(HALF, ids_ref[6:7, :] - HALF))
    queries, rows = (query(sources, relations), (high_ref[...], low_ref[...]))
    logits = dot3((high_across_ref[...], low_across_ref[...]), queries, NN)
    weights = relation_side(
        1, queries, sources, relations, rows, logits, ids_ref, counts_ref, mine_ref, other_ref, way_ref
    )
    dst_table, dst_state = target_update(queries, weights, dst_ref, dst_state_ref)
    upper_out[...] = dst_table[:CUT]
    lower_out[: W - CUT, :] = dst_table[CUT:]
    lower_out[W - CUT :, :] = jnp.broadcast_to(dst_state, (8, SLAB))


def last_kernel(
    way_ref, src_ref, src_state_ref, ids_ref, upper_ref, lower_ref, src_out, dst_out, dst_state_out, sem
):
    copies = [
        pltpu.make_async_copy(upper_ref, dst_out.at[pl.ds(0, CUT)], sem.at[0]),
        pltpu.make_async_copy(lower_ref.at[pl.ds(0, W - CUT)], dst_out.at[pl.ds(CUT, W - CUT)], sem.at[1]),
    ]
    for copy in copies:
        copy.start()
    dst_state_out[...] = lower_ref[W - CUT :, :][0]
    src_out[...], _ = source_update(1, way_ref, src_ref, src_state_ref, ids_ref)
    for copy in copies:
        copy.wait()


def call(kernel, outs, *args, scalars=0, scratch=(), passes=0, spaces=None):
    shapes = [shape if isinstance(shape, jax.ShapeDtypeStruct) else jax.ShapeDtypeStruct(shape, jnp.float32) for shape in outs]
    vector = pl.BlockSpec(memory_space=pltpu.VMEM)
    scalar = pl.BlockSpec(memory_space=pltpu.SMEM)
    moved = sum(value.size * value.dtype.itemsize for value in (*args, *shapes))
    return pl.pallas_call(
        kernel,
        out_shape=shapes,
        in_specs=[scalar] * scalars + [vector] * (len(args) - scalars),
        out_specs=spaces or [vector] * len(shapes),
        scratch_shapes=scratch,
        cost_estimate=pl.CostEstimate(flops=passes * 2 * EP * EP * SLAB, bytes_accessed=moved, transcendentals=0),
        compiler_params=pltpu.CompilerParams(vmem_limit_bytes=16 * 1024 * 1024),
    )(*args)


def shifted(value, steps):
    count = lax.axis_size(RIGHT)
    pairs = [(source, (source + steps) % count) for source in range(count)]
    return lax.ppermute(value, RIGHT, pairs)


def swapped(value):
    return lax.ppermute(value, "c", [(0, 1), (1, 0)])


def exchanged(value, axes):
    return lax.all_to_all(value, axes, split_axis=0, concat_axis=0, tiled=True)


def chip_half(mine, other):
    return mine + swapped(other)


def own_part(half):
    height = W // lax.axis_size(PLANE)
    return lax.dynamic_slice_in_dim(half, lax.axis_index(PLANE) * height, height, 0).reshape(-1)


def relation_update(half, own, own_sums, upper=None, lower=None, late=None):
    lanes, layers = (lax.axis_size(PLANE), lax.axis_size(COLUMN))
    total = jnp.sum(exchanged(half.reshape(lanes, 1, -1), PLANE), axis=(0, 1))
    if upper is not None:
        total, upper = lax.optimization_barrier((total, shifted(upper, -SHIFT)))
    total = jnp.sum(exchanged(jnp.broadcast_to(total, (layers, 1, *own.shape)), COLUMN), axis=(0, 1))
    if lower is not None:
        total, lower, late = lax.optimization_barrier((total, lower, late))
        lower = shifted(lower, -SHIFT)
    own_sums = own_sums + total * total
    own = own - REL_RATE * total / jnp.sqrt(own_sums)
    half = exchanged(jnp.broadcast_to(own, (lanes, 1, *own.shape)), PLANE).reshape(W, HALF)
    return (half, own, own_sums, upper, lower, late)


def padded(value, live, low):
    picked = value[low : low + BATCH]
    spot = lax.iota(jnp.int32, BATCH) + low
    return jnp.pad(jnp.where(spot < live, picked, -1), (0, EP - BATCH), constant_values=-1)


def body(
    src_embed, src_state, dst_embed, dst_state, relation, rel_state, edge_src, edge_dst, edge_rel, neg_rows, edge_count
):
    dst_table = shifted(dst_embed.T, SHIFT)
    core = lax.axis_index("c")
    live = edge_count[0]
    near_rel = edge_rel[0] ^ (core * HALF)
    ids = jnp.stack(
        [
            padded(edge_src[0], live, 0),
            padded(edge_src[0], live, BATCH),
            padded(edge_dst[0], live, 0),
            padded(edge_dst[0], live, BATCH),
            padded(edge_rel[0], live, 0),
            padded(near_rel, live, 0),
            padded(near_rel, live, BATCH),
            jnp.full((EP,), -1, jnp.int32),
        ]
    )
    negs = jnp.pad(neg_rows[0], ((0, 0), (0, NP - NEG)), constant_values=-1)
    place = core.reshape(1).astype(jnp.int32)
    src_table, src_sums = (src_embed.T, src_state.reshape(1, SLAB))

    flat = (1, SLAB)
    query_shapes = [jax.ShapeDtypeStruct((W, EP), jnp.bfloat16)] * 2
    weight_shapes = [jax.ShapeDtypeStruct((SLAB, EP), jnp.bfloat16)] * 2
    sources, relations, high, low, counts, own, own_sums, dst_sums = call(
        prepare_kernel,
        [(W, EP), (W, EP), *query_shapes, (SLAB, BATCHES), (W, HALF), (W, HALF), flat],
        place, src_table, relation.T, rel_state.T, ids, negs, dst_state.reshape(flat),
        scalars=1, passes=4,
    )
    dst_sums, own, own_sums = lax.optimization_barrier((dst_sums, own_part(own), own_part(own_sums)))
    dst_table, dst_sums = lax.optimization_barrier((dst_table, shifted(dst_sums, SHIFT)))
    mine, other, way, *weights = call(
        first_relation_kernel,
        [(W, HALF), (W, HALF), (W, EP), *weight_shapes],
        high, low, sources, relations, dst_table, ids, counts, passes=8,
    )
    half = chip_half(mine, other)
    half, *tables = lax.optimization_barrier(
        (
            half,
            *call(
                first_entity_kernel,
                [(W, SLAB), flat, (W, SLAB), flat],
                way, high, low, *weights, dst_table, dst_sums, src_table, src_sums, ids, passes=5,
            ),
        )
    )
    near, own, own_sums, *_ = relation_update(half, own, own_sums)
    near, src_table, src_sums, dst_table, dst_sums = lax.optimization_barrier((near, *tables))
    row_shapes = [jax.ShapeDtypeStruct((W, SLAB), jnp.bfloat16)] * 2 + [jax.ShapeDtypeStruct((SLAB, W), jnp.bfloat16)] * 2
    sources, *ready = call(
        gather_kernel, [(W, EP), (W, EP), *row_shapes], src_table, near, dst_table, ids, passes=3
    )
    near_rows, *rows = ready
    mine, other, way, upper, lower = call(
        second_kernel,
        [(W, HALF), (W, HALF), (W, EP), (CUT, SLAB), (W + 8 - CUT, SLAB)],
        swapped(near), near_rows, sources, *rows, dst_table, dst_sums, ids, counts, passes=13,
    )
    half = chip_half(mine, other)
    near, own, own_sums, upper, lower, way = relation_update(half, own, own_sums, upper, lower, way)
    near, lower = lax.optimization_barrier((near, lower))
    vector = pl.BlockSpec(memory_space=pltpu.VMEM)
    src_table, dst_table, dst_sums = call(
        last_kernel,
        [(W, SLAB), (W, SLAB), (SLAB,)],
        way, src_table, src_sums, ids, upper, lower,
        scratch=[pltpu.SemaphoreType.DMA((2,))], passes=2, spaces=[vector, pl.BlockSpec(memory_space=pl.ANY), vector],
    )
    far = swapped(near)
    first = core == 0
    relation = jnp.concatenate([jnp.where(first, near, far), jnp.where(first, far, near)], axis=1)
    return (src_table.T, dst_table.T, dst_sums, relation.T)


def solution(mesh):
    left, right = (mesh.shape["left"], mesh.shape["right"])
    devices = mesh.devices.reshape(left // 2, 2, 4, right // 8, 2)
    inner = Mesh(devices, AXES)
    in_specs = (
        P(AXES, None),
        P(AXES),
        P(AXES, None),
        P(AXES),
        P(),
        P(),
        P(AXES, None),
        P(AXES, None),
        P(AXES, None),
        P(AXES, None, None),
        P(AXES),
    )
    out_specs = (P(AXES, None), P(AXES, None), P(AXES), P())
    return jax.shard_map(body, mesh=inner, in_specs=in_specs, out_specs=out_specs, check_vma=False)
```

```python
import jax
import jax.numpy as jnp
from jax import lax
from jax.experimental import pallas as pl
from jax.experimental.pallas import tpu as pltpu
from jax.sharding import Mesh, PartitionSpec as P

BATCH = 500
BATCHES = 2
NEG = 1000
SHIFT = 5
SLAB = 384
REL = 256
HALF = 128
W = 400
MID = 200
EP = 512
NP = 1024
CUT = 200

ROW_RATE = 0.2
REL_RATE = 1.0

AXES = ("x", "zh", "y", "zl", "c")
PLANE = ("y", "x")
COLUMN = ("zl", "zh")
RIGHT = ("y", "zl", "c")

NN = (((1,), (0,)), ((), ()))
NT = (((1,), (1,)), ((), ()))
TN = (((0,), (0,)), ((), ()))


def parts(value):
    high = value.astype(jnp.bfloat16)
    low = (value - high.astype(jnp.float32)).astype(jnp.bfloat16)
    return (high, low)


def dot(first, second, dims):
    return lax.dot_general(first, second, dims, preferred_element_type=jnp.float32)


def joined(values, axis):
    return jnp.concatenate(values, axis=axis)


def dot3(first, second, dims):
    (one,), (two,) = dims[0]
    return dot(joined([first[0], first[0], first[1]], one), joined([second[0], second[1], second[0]], two), dims)


def pick(rows, ids):
    return (lax.broadcasted_iota(jnp.int32, (rows, EP), 0) == ids).astype(jnp.bfloat16)


def gather(table, hot):
    return dot(joined(parts(table), 1), joined([hot, hot], 0), NN)


def scatter(values, hot):
    high, low = parts(values)
    return dot(high, hot, NT) + dot(low, hot, NT)


def entity_update(table, state, grad):
    state = state + jnp.sum(grad * grad, axis=0, keepdims=True) * (1.0 / W)
    return (table - grad * (ROW_RATE / jnp.sqrt(state)), state)


def query(sources, relations):
    s_re, s_im = (sources[:MID], sources[MID:])
    r_re, r_im = (relations[:MID], relations[MID:])
    return parts(jnp.concatenate([s_re * r_re - s_im * r_im, s_re * r_im + s_im * r_re], axis=0))


def against(grads, other):
    g_re, g_im = (grads[:MID], grads[MID:])
    o_re, o_im = (other[:MID], other[MID:])
    return jnp.concatenate([g_re * o_re + g_im * o_im, g_im * o_re - g_re * o_im], axis=0)


def edge_weights(logits, dst_ids, counts):
    hit = lax.broadcasted_iota(jnp.int32, (SLAB, EP), 0) == dst_ids
    positive = jnp.where(hit, 0.5, 0.0)
    return parts((counts - positive) + (counts + positive) * jnp.tanh(0.5 * logits))


def put(refs, values):
    for ref, value in zip(refs, values, strict=True):
        ref[...] = value


def put(refs, values):
    for ref, value in zip(refs, values, strict=True):
        ref[...] = value


def relation_side(
    batch, queries, sources, relations, rows, logits, ids_ref, counts_ref, mine_ref, other_ref, way_ref
):
    dst_ids = ids_ref[2 + batch : 3 + batch, :]
    weights = edge_weights(logits, dst_ids, counts_ref[:, batch : batch + 1])
    grads = dot3(rows, weights, NN)
    rel_grad = scatter(against(grads, sources), pick(REL, ids_ref[5 + batch : 6 + batch, :]))
    put((mine_ref, other_ref), (rel_grad[:, :HALF], rel_grad[:, HALF:]))
    way_ref[...] = against(grads, relations)
    return weights


def target_update(queries, weights, dst_ref, dst_state_ref):
    return entity_update(dst_ref[...], dst_state_ref[...], dot3(queries, weights, NT))


def source_update(batch, way_ref, src_ref, src_state_ref, ids_ref):
    src_grad = scatter(way_ref[...], pick(SLAB, ids_ref[batch : batch + 1, :]))
    return entity_update(src_ref[...], src_state_ref[...], src_grad)


def prepare_kernel(
    place_ref, src_ref, rel_ref, rel_state_ref, ids_ref, neg_ref, dst_state_ref,
    sources_ref, relations_ref, high_ref, low_ref, counts_ref, own_ref, own_sums_ref, dst_state_out,
):
    sources = gather(src_ref[...], pick(SLAB, ids_ref[0:1, :]))
    relations = gather(rel_ref[...], pick(REL, ids_ref[4:5, :]))
    put((sources_ref, relations_ref), (sources, relations))
    put((high_ref, low_ref), query(sources, relations))
    for batch in range(BATCHES):
        same = lax.broadcasted_iota(jnp.int32, (SLAB, NP), 0) == neg_ref[batch : batch + 1, :]
        total = jnp.sum(jnp.where(same, 1.0, 0.0), axis=1, keepdims=True)
        counts_ref[:, batch : batch + 1] = total * (0.5 / NEG)
    for source, target in ((rel_ref, own_ref), (rel_state_ref, own_sums_ref)):
        target[...] = jnp.where(place_ref[0] == 0, source[:, :HALF], source[:, HALF:])
    dst_state_out[...] = dst_state_ref[...]


def first_relation_kernel(
    high_ref, low_ref, sources_ref, relations_ref, dst_ref, ids_ref, counts_ref, mine_ref, other_ref, way_ref, *weight_refs
):
    queries, rows = ((high_ref[...], low_ref[...]), parts(dst_ref[...]))
    weights = relation_side(
        0, queries, sources_ref[...], relations_ref[...], rows, dot3(rows, queries, TN), ids_ref, counts_ref,
        mine_ref, other_ref, way_ref,
    )
    put(weight_refs, weights)


def first_entity_kernel(
    way_ref, high_ref, low_ref, weight_high_ref, weight_low_ref, dst_ref, dst_state_ref, src_ref, src_state_ref, ids_ref,
    src_out, src_state_out, dst_out, dst_state_out,
):
    src_out[...], src_state_out[...] = source_update(0, way_ref, src_ref, src_state_ref, ids_ref)
    queries, weights = ((high_ref[...], low_ref[...]), (weight_high_ref[...], weight_low_ref[...]))
    dst_out[...], dst_state_out[...] = target_update(queries, weights, dst_ref, dst_state_ref)


def gather_kernel(src_ref, near_ref, dst_ref, ids_ref, sources_ref, near_rows_ref, *row_refs):
    sources_ref[...] = gather(src_ref[...], pick(SLAB, ids_ref[1:2, :]))
    near_rows_ref[...] = gather(near_ref[...], pick(HALF, ids_ref[6:7, :]))
    rows = parts(dst_ref[...])
    put(row_refs, (*rows, *[jnp.transpose(part) for part in rows]))


def second_kernel(
    far_ref, near_rows_ref, sources_ref, high_ref, low_ref, high_across_ref, low_across_ref, dst_ref, dst_state_ref,
    ids_ref, counts_ref, mine_ref, other_ref, way_ref, upper_out, lower_out,
):
    sources = sources_ref[...]
    relations = near_rows_ref[...] + gather(far_ref[...], pick(HALF, ids_ref[6:7, :] - HALF))
    queries, rows = (query(sources, relations), (high_ref[...], low_ref[...]))
    logits = dot3((high_across_ref[...], low_across_ref[...]), queries, NN)
    weights = relation_side(
        1, queries, sources, relations, rows, logits, ids_ref, counts_ref, mine_ref, other_ref, way_ref
    )
    dst_table, dst_state = target_update(queries, weights, dst_ref, dst_state_ref)
    upper_out[...] = dst_table[:CUT]
    lower_out[: W - CUT, :] = dst_table[CUT:]
    lower_out[W - CUT :, :] = jnp.broadcast_to(dst_state, (8, SLAB))


def last_kernel(
    way_ref, src_ref, src_state_ref, ids_ref, upper_ref, lower_ref, src_out, dst_out, dst_state_out, sem
):
    copies = [
        pltpu.make_async_copy(upper_ref, dst_out.at[pl.ds(0, CUT)], sem.at[0]),
        pltpu.make_async_copy(lower_ref.at[pl.ds(0, W - CUT)], dst_out.at[pl.ds(CUT, W - CUT)], sem.at[1]),
    ]
    for copy in copies:
        copy.start()
    dst_state_out[...] = lower_ref[W - CUT :, :][0]
    src_out[...], _ = source_update(1, way_ref, src_ref, src_state_ref, ids_ref)
    for copy in copies:
        copy.wait()


def call(kernel, outs, *args, scalars=0, scratch=(), passes=0, spaces=None):
    shapes = [shape if isinstance(shape, jax.ShapeDtypeStruct) else jax.ShapeDtypeStruct(shape, jnp.float32) for shape in outs]
    vector = pl.BlockSpec(memory_space=pltpu.VMEM)
    scalar = pl.BlockSpec(memory_space=pltpu.SMEM)
    moved = sum(value.size * value.dtype.itemsize for value in (*args, *shapes))
    return pl.pallas_call(
        kernel,
        out_shape=shapes,
        in_specs=[scalar] * scalars + [vector] * (len(args) - scalars),
        out_specs=spaces or [vector] * len(shapes),
        scratch_shapes=scratch,
        cost_estimate=pl.CostEstimate(flops=passes * 2 * EP * EP * SLAB, bytes_accessed=moved, transcendentals=0),
        compiler_params=pltpu.CompilerParams(vmem_limit_bytes=16 * 1024 * 1024),
    )(*args)


def shifted(value, steps):
    count = lax.axis_size(RIGHT)
    pairs = [(source, (source + steps) % count) for source in range(count)]
    return lax.ppermute(value, RIGHT, pairs)


def swapped(value):
    return lax.ppermute(value, "c", [(0, 1), (1, 0)])


def exchanged(value, axes):
    return lax.all_to_all(value, axes, split_axis=0, concat_axis=0, tiled=True)


def chip_half(mine, other):
    return mine + swapped(other)


def own_part(half):
    height = W // lax.axis_size(PLANE)
    return lax.dynamic_slice_in_dim(half, lax.axis_index(PLANE) * height, height, 0).reshape(-1)


def relation_update(half, own, own_sums, upper=None, lower=None, late=None):
    lanes, layers = (lax.axis_size(PLANE), lax.axis_size(COLUMN))
    total = jnp.sum(exchanged(half.reshape(lanes, 1, -1), PLANE), axis=(0, 1))
    if upper is not None:
        total, upper = lax.optimization_barrier((total, shifted(upper, -SHIFT)))
    total = jnp.sum(exchanged(jnp.broadcast_to(total, (layers, 1, *own.shape)), COLUMN), axis=(0, 1))
    if lower is not None:
        total, lower, late = lax.optimization_barrier((total, lower, late))
        lower = shifted(lower, -SHIFT)
    own_sums = own_sums + total * total
    own = own - REL_RATE * total / jnp.sqrt(own_sums)
    half = exchanged(jnp.broadcast_to(own, (lanes, 1, *own.shape)), PLANE).reshape(W, HALF)
    return (half, own, own_sums, upper, lower, late)


def padded(value, live, low):
    picked = value[low : low + BATCH]
    spot = lax.iota(jnp.int32, BATCH) + low
    return jnp.pad(jnp.where(spot < live, picked, -1), (0, EP - BATCH), constant_values=-1)


def body(
    src_embed, src_state, dst_embed, dst_state, relation, rel_state, edge_src, edge_dst, edge_rel, neg_rows, edge_count
):
    dst_table = shifted(dst_embed.T, SHIFT)
    core = lax.axis_index("c")
    live = edge_count[0]
    near_rel = edge_rel[0] ^ (core * HALF)
    ids = jnp.stack(
        [
            padded(edge_src[0], live, 0),
            padded(edge_src[0], live, BATCH),
            padded(edge_dst[0], live, 0),
            padded(edge_dst[0], live, BATCH),
            padded(edge_rel[0], live, 0),
            padded(near_rel, live, 0),
            padded(near_rel, live, BATCH),
            jnp.full((EP,), -1, jnp.int32),
        ]
    )
    negs = jnp.pad(neg_rows[0], ((0, 0), (0, NP - NEG)), constant_values=-1)
    place = core.reshape(1).astype(jnp.int32)
    src_table, src_sums = (src_embed.T, src_state.reshape(1, SLAB))

    flat = (1, SLAB)
    query_shapes = [jax.ShapeDtypeStruct((W, EP), jnp.bfloat16)] * 2
    weight_shapes = [jax.ShapeDtypeStruct((SLAB, EP), jnp.bfloat16)] * 2
    sources, relations, high, low, counts, own, own_sums, dst_sums = call(
        prepare_kernel,
        [(W, EP), (W, EP), *query_shapes, (SLAB, BATCHES), (W, HALF), (W, HALF), flat],
        place, src_table, relation.T, rel_state.T, ids, negs, dst_state.reshape(flat),
        scalars=1, passes=4,
    )
    dst_sums, own, own_sums = lax.optimization_barrier((dst_sums, own_part(own), own_part(own_sums)))
    dst_table, dst_sums = lax.optimization_barrier((dst_table, shifted(dst_sums, SHIFT)))
    mine, other, way, *weights = call(
        first_relation_kernel,
        [(W, HALF), (W, HALF), (W, EP), *weight_shapes],
        high, low, sources, relations, dst_table, ids, counts, passes=8,
    )
    half = chip_half(mine, other)
    half, *tables = lax.optimization_barrier(
        (
            half,
            *call(
                first_entity_kernel,
                [(W, SLAB), flat, (W, SLAB), flat],
                way, high, low, *weights, dst_table, dst_sums, src_table, src_sums, ids, passes=5,
            ),
        )
    )
    near, own, own_sums, *_ = relation_update(half, own, own_sums)
    near, src_table, src_sums, dst_table, dst_sums = lax.optimization_barrier((near, *tables))
    row_shapes = [jax.ShapeDtypeStruct((W, SLAB), jnp.bfloat16)] * 2 + [jax.ShapeDtypeStruct((SLAB, W), jnp.bfloat16)] * 2
    sources, *ready = call(
        gather_kernel, [(W, EP), (W, EP), *row_shapes], src_table, near, dst_table, ids, passes=3
    )
    near_rows, *rows = ready
    mine, other, way, upper, lower = call(
        second_kernel,
        [(W, HALF), (W, HALF), (W, EP), (CUT, SLAB), (W + 8 - CUT, SLAB)],
        swapped(near), near_rows, sources, *rows, dst_table, dst_sums, ids, counts, passes=13,
    )
    half = chip_half(mine, other)
    near, own, own_sums, upper, lower, way = relation_update(half, own, own_sums, upper, lower, way)
    near, lower = lax.optimization_barrier((near, lower))
    vector = pl.BlockSpec(memory_space=pltpu.VMEM)
    src_table, dst_table, dst_sums = call(
        last_kernel,
        [(W, SLAB), (W, SLAB), (SLAB,)],
        way, src_table, src_sums, ids, upper, lower,
        scratch=[pltpu.SemaphoreType.DMA((2,))], passes=2, spaces=[vector, pl.BlockSpec(memory_space=pl.ANY), vector],
    )
    far = swapped(near)
    relation = jnp.zeros((W, REL), jnp.float32)
    relation = lax.dynamic_update_slice_in_dim(relation, near, core * HALF, 1)
    relation = lax.dynamic_update_slice_in_dim(relation, far, (1 - core) * HALF, 1)
    return (src_table.T, dst_table.T, dst_sums, relation.T)


def solution(mesh):
    left, right = (mesh.shape["left"], mesh.shape["right"])
    devices = mesh.devices.reshape(left // 2, 2, 4, right // 8, 2)
    inner = Mesh(devices, AXES)
    in_specs = (
        P(AXES, None),
        P(AXES),
        P(AXES, None),
        P(AXES),
        P(),
        P(),
        P(AXES, None),
        P(AXES, None),
        P(AXES, None),
        P(AXES, None, None),
        P(AXES),
    )
    out_specs = (P(AXES, None), P(AXES, None), P(AXES), P())
    return jax.shard_map(body, mesh=inner, in_specs=in_specs, out_specs=out_specs, check_vma=False)
```
